128 devices in a mesh: elem: 32 (over z, y, core), span: 4 (over x).
Axes of the slice: x: 4, y: 4, z: 4, core: 2. Of those that a mesh axis runs over, the one named last changes fastest.
Arguments:
- state: float32 [512, 32, 128], P('elem', 'span'), may hold values from -6 to 6
- assignment: int32 [512, 32], P('elem', 'span'), may hold values from 0 to 32767, as said below
- surface: bfloat16 [32768, 16], P(('elem', 'span')), may hold values from -6 to 6
- w_state: bfloat16 [4, 2048], replicated, may hold values from -3 to 3
- w_surf: bfloat16 [16, 2048], replicated, may hold values from -1.5 to 1.5
- w_hidden: bfloat16 [512, 2048], replicated, may hold values from -0.25 to 0.25
- bias: float32 [2048], replicated, may hold values from -3 to 3
- w_out: bfloat16 [512, 4], replicated, may hold values from -0.25 to 0.25
Outputs:
- new_state: float32 [512, 32, 128], P('elem', 'span')
The draws below stay inside these ranges and needn't reach their ends.
Inputs may be any that keep to these rules, and one draw needn't show every extreme that they name: `assignment`: each value is a physics device index (elem index times the span axis size plus span index) times 256 plus a slot below 256. No two columns share a value. The columns of one device take at most 2 slots of any one physics device, and every device takes 2 slots of some physics device; some physics device has all 256 slots taken.
All inputs are finite; a program needn't handle non-finite values.
Results may differ from the reference program's by a relative error of at most 0.0017.
Values may be sent and summed in bfloat16 or wider, within the bound.
No kernel may reach another device: no remote copies, remote signals or barrier semaphores. Data moves between devices by JAX's collectives and lax.ppermute only.
A program may use at most 64 MiB of HBM per device.

```python
import math
import jax
import jax.numpy as jnp
import numpy as np
from jax import lax

NP = 4
NV = 4
HID = 512
NS = 16
SUBSTEPS = 2
PX = 16
PY = 8
COLS = 128
PCAP = 256
NXP = 512
NYP = 32
PHYS = 32768
CHAN = 128
GATES = 2048
N_ELEM = 32
N_SPAN = 4


def draw_assignment(key, part):
    key = jax.random.fold_in(key, 7)
    key_order, key_start, key_cols = jax.random.split(key, 3)
    devices = N_ELEM * N_SPAN
    cap = 2 * COLS // devices
    heavy_count = devices // 4
    light_count = devices - heavy_count
    order = jax.random.permutation(key_order, devices).astype(jnp.int32)
    starts = jax.random.randint(key_start, (devices,), 0, light_count).astype(jnp.int32)
    steps_light = jnp.arange(devices // 4, dtype=jnp.int32)
    light_pick = order[heavy_count + (starts[:, None] + steps_light[None, :]) % light_count]
    heavy_pick = jnp.broadcast_to(order[:heavy_count][None, :], (devices, heavy_count))
    picks = jnp.concatenate([heavy_pick, light_pick], axis=1).astype(jnp.int32)
    sources = jnp.arange(devices, dtype=jnp.int32)[:, None]
    chosen = jnp.zeros((devices, devices), jnp.int32).at[sources, picks].set(1)
    before = jnp.cumsum(chosen, axis=0) - chosen
    offsets = jnp.take_along_axis(before, picks, axis=1) * cap
    ranks = jnp.arange(COLS, dtype=jnp.int32)
    groups = ranks // cap
    within = ranks % cap
    slots = picks[:, groups] * PCAP + offsets[:, groups] + within[None, :]
    shuffles = jax.vmap(lambda piece: jax.random.permutation(piece, COLS))(jax.random.split(key_cols, devices))
    placed = jax.vmap(lambda order_cols, values: jnp.zeros((COLS,), jnp.int32).at[order_cols].set(values))(shuffles, slots)
    laid = placed.reshape(N_ELEM, N_SPAN, PX, PY).transpose(0, 2, 1, 3).reshape(N_ELEM * PX, N_SPAN * PY)
    return laid.astype(jnp.int32)


def level_of(own_key, shape, cuts, low, largest):
    factor_of = 1.0
    for dim, blocks in cuts:
        heights = jax.random.uniform(jax.random.fold_in(jax.random.fold_in(own_key, 6), dim), (blocks,), jnp.float32, low / len(cuts), largest / len(cuts))
        factor_of = factor_of * jnp.repeat(jnp.exp(heights), shape[dim] // blocks).reshape((-1,) + (1,) * (len(shape) - 1 - dim))
    return factor_of


def noise(own_key, dims, scale, limit, cuts=(), kind=jnp.bfloat16):
    values = scale * jax.random.normal(own_key, dims, jnp.float32)
    if cuts:
        values = values * level_of(own_key, dims, cuts, -0.22, 0.18)
    return jnp.clip(values, -limit, limit).astype(kind)


def setup_inputs(seed: int = 0) -> dict:
    splits = jax.random.split(jax.random.key(seed), 9)
    state = noise(splits[0], (NXP, NYP, CHAN), 1.0, 6.0, ((0, 32), (1, 4)), jnp.float32)
    assignment = draw_assignment(jax.random.fold_in(splits[8], 71), 0)
    surface = noise(splits[2], (PHYS, NS), 1.0, 6.0, ((0, 128),))
    w_state = noise(splits[3], (NV, GATES), NV ** -0.5, 3.0)
    w_surf = noise(splits[4], (NS, GATES), NS ** -0.5, 1.5)
    w_hidden = noise(splits[5], (HID, GATES), HID ** -0.5, 0.25)
    bias = noise(splits[6], (GATES,), 0.5, 3.0, (), jnp.float32)
    w_out = noise(splits[7], (HID, NV), HID ** -0.5, 0.25)
    return {"state": state, "assignment": assignment, "surface": surface, "w_state": w_state, "w_surf": w_surf, "w_hidden": w_hidden, "bias": bias, "w_out": w_out}


courant = 0.05

def gll_table():
    nodes = np.array([-1.0, -1.0 / math.sqrt(5.0), 1.0 / math.sqrt(5.0), 1.0])
    width = nodes.shape[0]
    table = np.zeros((width, width))
    for row in range(width):
        for column in range(width):
            if row != column:
                upper = np.prod([nodes[row] - nodes[other] for other in range(width) if other != row])
                lower = np.prod([nodes[column] - nodes[other] for other in range(width) if other != column])
                table[row, column] = upper / (lower * (nodes[row] - nodes[column]))
            else:
                table[row, row] = sum((1.0 / (nodes[row] - nodes[other]) for other in range(width) if other != row))
    return table

def derivative(grid, position):
    table = gll_table()
    pieces = []
    for row in range(NP):
        total = None
        for column in range(NP):
            term = float(table[row, column]) * lax.index_in_dim(grid, column, position, keepdims=False)
            total = term if total is None else total + term
        pieces.append(total)
    return jnp.stack(pieces, axis=position)

def advect(field):
    rows, columns, channels = field.shape
    grid = field.reshape(rows // NP, NP, columns // NP, NP, channels // NV, NV)
    along_x = derivative(grid, 1)
    along_y = derivative(grid, 3)
    wind_x = grid[..., 0:1]
    wind_y = grid[..., 1:2]
    moved = grid - courant * (wind_x * along_x + wind_y * along_y)
    return moved.reshape(rows, columns, channels)

def average_edges(padded):
    rows = padded.shape[0] - 2
    middle = padded[1:-1]
    position = (jnp.arange(rows) % NP)[:, None, None]
    first = jnp.where(position == NP - 1, (middle + padded[2:]) * 0.5, jnp.where(position == 0, (middle + padded[:-2]) * 0.5, middle))
    columns = first.shape[1] - 2
    centre = first[:, 1:-1]
    place = (jnp.arange(columns) % NP)[None, :, None]
    return jnp.where(place == NP - 1, (centre + first[:, 2:]) * 0.5, jnp.where(place == 0, (centre + first[:, :-2]) * 0.5, centre))

def imitate(columns, surf, w_state, w_surf, w_hidden, bias, w_out):
    rows = columns.shape[0]
    levels = columns.shape[1] // NV
    hidden_size = w_hidden.shape[0]
    base = jnp.dot(surf, w_surf, preferred_element_type=jnp.float32) + bias
    inputs = jnp.transpose(columns.reshape(rows, levels, NV), (1, 0, 2))

    def advance(carry, level_in):
        hidden, cell = carry
        gates = base + jnp.dot(level_in, w_state, preferred_element_type=jnp.float32) + jnp.dot(hidden, w_hidden, preferred_element_type=jnp.float32)
        inner, forget, candidate, output = jnp.split(gates, 4, axis=1)
        cell = jax.nn.sigmoid(forget) * cell + jax.nn.sigmoid(inner) * jnp.tanh(candidate)
        hidden = (jax.nn.sigmoid(output) * jnp.tanh(cell)).astype(jnp.bfloat16)
        return ((hidden, cell), jnp.dot(hidden, w_out, preferred_element_type=jnp.float32))
    start = (jnp.zeros((rows, hidden_size), jnp.bfloat16), jnp.zeros((rows, hidden_size), jnp.float32))
    _, outputs = lax.scan(advance, start, inputs)
    return jnp.transpose(outputs, (1, 0, 2)).reshape(rows, levels * NV).astype(jnp.bfloat16)

def reference(state, assignment, surface, w_state, w_surf, w_hidden, bias, w_out):
    field = state
    for substep in range(SUBSTEPS):
        field = advect(field)
        padded = jnp.pad(field, ((1, 1), (1, 1), (0, 0)), mode='wrap')
        field = average_edges(padded)
    total = NXP * NYP
    columns = field.reshape(total, CHAN).astype(jnp.bfloat16)
    surf_rows = jnp.take(surface, assignment.reshape(total).astype(jnp.int32), axis=0)
    block = math.gcd(total, 4096)

    def one_block(pair):
        return imitate(pair[0], pair[1], w_state, w_surf, w_hidden, bias, w_out)
    tendency = lax.map(one_block, (columns.reshape(total // block, block, CHAN), surf_rows.reshape(total // block, block, NS)))
    return field + tendency.reshape(NXP, NYP, CHAN).astype(jnp.float32)
```

```python
import math

import jax
import jax.numpy as jnp
import numpy as np
from jax import lax
from jax.experimental import pallas as pl
from jax.experimental.pallas import tpu as pltpu
from jax.sharding import PartitionSpec as P

NP = 4
NV = 4
HID = 512
LEVELS = 32
LANES = 128
COURANT = 0.05
F32 = jnp.float32
BF16 = jnp.bfloat16
VMEM_LIMIT = 48 << 20


def gll_table():
    nodes = np.array([-1.0, -1.0 / math.sqrt(5.0), 1.0 / math.sqrt(5.0), 1.0])
    width = nodes.shape[0]
    table = np.zeros((width, width))
    for row in range(width):
        for column in range(width):
            if row != column:
                upper = np.prod(
                    [nodes[row] - nodes[other] for other in range(width) if other != row]
                )
                lower = np.prod(
                    [nodes[column] - nodes[other] for other in range(width) if other != column]
                )
                table[row, column] = upper / (lower * (nodes[row] - nodes[column]))
            else:
                table[row, row] = sum(
                    (1.0 / (nodes[row] - nodes[other]) for other in range(width) if other != row)
                )
    return table


D = [[float(v) for v in row] for row in gll_table()]


def winds(f):
    flat = f.reshape(-1, LANES)
    v = lax.broadcasted_iota(jnp.int32, flat.shape, 1) % NV
    one = pltpu.roll(flat, 1, 1)
    two = pltpu.roll(flat, 2, 1)
    three = pltpu.roll(flat, 3, 1)
    back = pltpu.roll(flat, LANES - 1, 1)
    first = jnp.where(v == 0, flat, jnp.where(v == 1, one, jnp.where(v == 2, two, three)))
    second = jnp.where(v == 0, back, jnp.where(v == 1, flat, jnp.where(v == 2, one, two)))
    return first.reshape(f.shape), second.reshape(f.shape)


def along_x(f):
    rows = f.reshape(f.shape[0] // NP, NP, f.shape[1], LANES)
    pieces = []
    for i in range(NP):
        total = D[i][0] * rows[:, 0]
        for k in range(1, NP):
            total = total + D[i][k] * rows[:, k]
        pieces.append(total)
    return jnp.stack(pieces, axis=1).reshape(f.shape)


def along_y(f):
    size = f.shape[1]
    y = lax.broadcasted_iota(jnp.int32, (1, size, LANES), 1) % NP
    total = None
    for shift in range(-(NP - 1), NP):
        factor = jnp.zeros((1, size, LANES), F32)
        for i in range(NP):
            if 0 <= i + shift < NP:
                factor = jnp.where(y == i, D[i][i + shift], factor)
        moved = f if shift == 0 else pltpu.roll(f, (-shift) % size, 1)
        term = factor * moved
        total = term if total is None else total + term
    return total


def average_y(f, left, right):
    size = f.shape[1]
    y = lax.broadcasted_iota(jnp.int32, (1, size, LANES), 1)
    ahead = pltpu.roll(f, size - 1, 1)
    behind = pltpu.roll(f, 1, 1)
    other = jnp.where(y % NP == NP - 1, ahead, jnp.where(y % NP == 0, behind, f))
    other = jnp.where(y == size - 1, right, jnp.where(y == 0, left, other))
    return (f + other) * 0.5


def average_x(f, before, after):
    rows = f.shape[0]
    pieces = []
    for r in range(rows):
        if r % NP == 0:
            other = before if r == 0 else f[r - 1]
            pieces.append((f[r] + other) * 0.5)
        elif r % NP == NP - 1:
            other = after if r == rows - 1 else f[r + 1]
            pieces.append((f[r] + other) * 0.5)
        else:
            pieces.append(f[r])
    return jnp.stack(pieces, axis=0)


def first_kernel(state_ref, moved_ref, to_before_ref, to_after_ref):
    f = state_ref[...]
    wind_x, wind_y = winds(f)
    a = f - COURANT * (wind_x * along_x(f) + wind_y * along_y(f))
    moved_ref[...] = a
    n = a.shape[0]
    to_before_ref[0] = a[0]
    to_before_ref[1] = D[0][1] * a[1] + D[0][2] * a[2] + D[0][3] * ((a[3] + a[4]) * 0.5)
    to_after_ref[0] = a[n - 1]
    to_after_ref[1] = (
        D[3][0] * ((a[n - 4] + a[n - 5]) * 0.5) + D[3][1] * a[n - 3] + D[3][2] * a[n - 2]
    )


def second_kernel(moved_ref, before_ref, after_ref, g_ref, to_left_ref, to_right_ref):
    g = average_x(moved_ref[...], before_ref[0], after_ref[0])
    g_ref[...] = g
    rows, size, _ = g.shape
    middle = (g[:, 3] + g[:, 4]) * 0.5
    to_left_ref[0:rows] = g[:, 0]
    to_left_ref[rows : 2 * rows] = D[0][1] * g[:, 1] + D[0][2] * g[:, 2] + D[0][3] * middle
    to_right_ref[0:rows] = g[:, size - 1]
    to_right_ref[rows : 2 * rows] = (
        D[3][0] * middle + D[3][1] * g[:, size - 3] + D[3][2] * g[:, size - 2]
    )
    up, down = before_ref[1], after_ref[1]
    y = lax.broadcasted_iota(jnp.int32, (size, LANES), 0)
    to_left_ref[2 * rows : 2 * rows + 8] = jnp.where(
        y == 0, up, jnp.where(y == 1, pltpu.roll(down, 1, 0), 0.0)
    )
    to_right_ref[2 * rows : 2 * rows + 8] = jnp.where(
        y == 0, pltpu.roll(up, 1, 0), jnp.where(y == 1, pltpu.roll(down, 2, 0), 0.0)
    )


def third_kernel(g_ref, before_ref, after_ref, left_ref, right_ref, field_ref):
    g = g_ref[...]
    rows, size, _ = g.shape
    left_g = left_ref[0:rows].reshape(rows, 1, LANES)
    right_g = right_ref[0:rows].reshape(rows, 1, LANES)
    f = average_y(g, left_g, right_g)
    tail_l = left_ref[2 * rows : 2 * rows + 8]
    tail_r = right_ref[2 * rows : 2 * rows + 8]
    up = average_y(before_ref[1:2], tail_l[0:1].reshape(1, 1, LANES), tail_r[0:1].reshape(1, 1, LANES))[0]
    down = average_y(after_ref[1:2], tail_l[1:2].reshape(1, 1, LANES), tail_r[1:2].reshape(1, 1, LANES))[0]
    slope_x = average_x(
        along_x(f), D[3][3] * f[0] + up, D[0][0] * f[rows - 1] + down
    )
    other_l = left_ref[rows : 2 * rows].reshape(rows, 1, LANES)
    other_r = right_ref[rows : 2 * rows].reshape(rows, 1, LANES)
    slope_y = average_y(along_y(f), D[3][3] * f + other_l, D[0][0] * f + other_r)
    wind_x, wind_y = winds(f)
    field_ref[...] = f - COURANT * (wind_x * slope_x + wind_y * slope_y)


def weights_kernel(state_w_ref, surf_w_ref, hidden_w_ref, bias_ref, out_w_ref, w_ref, o_ref):
    lane = lax.broadcasted_iota(jnp.int32, (1, 4 * HID), 1)
    scale = jnp.where((lane >= 2 * HID) & (lane < 3 * HID), 1.0, 0.5)
    w_ref[0:HID] = (hidden_w_ref[...].astype(F32) * scale).astype(BF16)
    row = lax.broadcasted_iota(jnp.int32, (64, NV), 0)
    col = lax.broadcasted_iota(jnp.int32, (64, NV), 1)
    spread = (row % NV == col).astype(BF16)
    tiled = jnp.dot(spread, state_w_ref[...], preferred_element_type=F32)
    w_ref[HID : HID + 64] = (tiled * scale).astype(BF16)
    rest = bias_ref[...] * scale
    high = rest.astype(BF16).astype(F32)
    rest = rest - high
    mid = rest.astype(BF16).astype(F32)
    low = rest - mid
    r = lax.broadcasted_iota(jnp.int32, (16, 1), 0)
    parts = jnp.where(r == 0, high, jnp.where(r == 1, mid, jnp.where(r == 2, low, 0.0)))
    w_ref[HID + 64 : HID + 80] = parts.astype(BF16)
    w_ref[HID + 80 : HID + 96] = (surf_w_ref[...].astype(F32) * scale).astype(BF16)
    w_ref[HID + 96 : HID + 128] = jnp.zeros((32, 4 * HID), BF16)
    row = lax.broadcasted_iota(jnp.int32, (NV, LANES), 0)
    col = lax.broadcasted_iota(jnp.int32, (NV, LANES), 1)
    spread = (col % NV == row).astype(BF16)
    o_ref[...] = jnp.dot(out_w_ref[...], spread, preferred_element_type=F32).astype(BF16)


def lstm_kernel(slots_ref, table_ref, field_ref, w_ref, o_ref, out_ref, cell_ref, gain_ref):
    rows = field_ref.shape[0]
    feature_lane = lax.broadcasted_iota(jnp.int32, (16, LANES), 1)

    def fetch(c, acc):
        slot = slots_ref[c]
        owner = lax.shift_right_logical(slot, 8)
        place = jnp.bitwise_and(slot, 255)
        half = pl.multiple_of(jnp.bitwise_and(place, 128), 128)
        tile = table_ref[owner, :, pl.ds(half, LANES)].astype(F32)
        shift = jnp.bitwise_and(c - place + 256, 127)
        return jnp.where(feature_lane == c, pltpu.roll(tile, shift, 1), acc)

    surf = lax.fori_loop(0, rows, fetch, jnp.zeros((16, LANES), F32), unroll=8)
    surf = jnp.concatenate(
        [jnp.zeros((80, LANES), F32), surf, jnp.zeros((32, LANES), F32)], axis=0
    ).T
    lane = lax.broadcasted_iota(jnp.int32, (rows, LANES), 1)
    fixed = jnp.where((lane >= 64) & (lane < 67), 1.0, surf)
    field = field_ref[...]
    swapped = pltpu.roll(field, 64, 1)
    unit = 256

    def level_input(level):
        source = jnp.where(level < LEVELS // 2, field, swapped)
        return jnp.where(lane // NV == level % (LEVELS // 2), source, fixed).astype(BF16)

    def gates(x, h, j):
        out = []
        for q in range(4):
            s = slice(q * HID + j * unit, q * HID + (j + 1) * unit)
            g = jnp.dot(x, w_ref[HID : HID + LANES, s], preferred_element_type=F32)
            if h is not None:
                g = g + jnp.dot(h, w_ref[0:HID, s], preferred_element_type=F32)
            out.append(g)
        return out

    def cell_step(g, j, first):
        s = slice(j * unit, (j + 1) * unit)
        c = (0.5 * jnp.tanh(g[0]) + 0.5) * jnp.tanh(g[2])
        if not first:
            c = c + (0.5 * jnp.tanh(g[1]) + 0.5) * cell_ref[:, s]
        cell_ref[:, s] = c
        return ((0.5 * jnp.tanh(g[3]) + 0.5) * jnp.tanh(c)).astype(BF16)

    def emit(h, level):
        p = jnp.dot(h, o_ref[...], preferred_element_type=F32)
        gain_ref[...] = jnp.where(lane // NV == level, p, gain_ref[...])

    def step(level, h, first=False):
        x = level_input(level)
        new = [cell_step(gates(x, h, j), j, first) for j in range(HID // unit)]
        new = jnp.concatenate(new, axis=1)
        emit(new, level)
        return new

    gain_ref[...] = jnp.zeros_like(gain_ref)
    h = step(0, None, True)
    lax.fori_loop(1, LEVELS, step, h)
    out_ref[...] = field + gain_ref[...].astype(BF16).astype(F32)


def call(kernel, out_shape, *args, smem=(), scratch=(), cost=None):
    return pl.pallas_call(
        kernel,
        out_shape=out_shape,
        in_specs=[
            pl.BlockSpec(memory_space=pltpu.SMEM if i in smem else pltpu.VMEM)
            for i in range(len(args))
        ],
        out_specs=jax.tree.map(lambda _: pl.BlockSpec(memory_space=pltpu.VMEM), out_shape),
        scratch_shapes=list(scratch),
        compiler_params=pltpu.CompilerParams(vmem_limit_bytes=VMEM_LIMIT),
        cost_estimate=cost,
    )(*args)


def like(*shape, dtype=F32):
    return jax.ShapeDtypeStruct(shape, dtype)


def exchange(to_lower, to_upper, axis):
    size = lax.axis_size(axis)
    up = [(i, (i + 1) % size) for i in range(size)]
    down = [(j, i) for i, j in up]
    return lax.ppermute(to_upper, axis, up), lax.ppermute(to_lower, axis, down)


def shards(state, assignment, surface, w_state, w_surf, w_hidden, bias, w_out):
    node_rows, node_cols, channels = state.shape
    devices = lax.axis_size("elem") * lax.axis_size("span")
    columns_here = node_rows * node_cols
    slot_count, features = surface.shape
    table = lax.all_to_all(
        jnp.broadcast_to(surface.T[None], (devices, features, slot_count)),
        ("elem", "span"),
        split_axis=0,
        concat_axis=0,
        tiled=True,
    )
    block = like(node_rows, node_cols, channels)
    edge = like(2, node_cols, channels)
    moved, to_before, to_after = call(first_kernel, (block, edge, edge), state)
    before, after = exchange(to_before, to_after, "elem")
    side = like(2 * node_rows + 8, channels)
    g, to_left, to_right = call(second_kernel, (block, side, side), moved, before, after)
    left, right = exchange(to_left, to_right, "span")
    field = call(third_kernel, block, g, before, after, left, right)
    weights, out_weights = call(
        weights_kernel,
        (like(HID + LANES, 4 * HID, dtype=BF16), like(HID, LANES, dtype=BF16)),
        w_state,
        w_surf,
        w_hidden,
        bias.reshape(1, 4 * HID),
        w_out,
    )
    result = call(
        lstm_kernel,
        like(columns_here, channels),
        assignment.reshape(columns_here),
        table,
        field.reshape(columns_here, channels),
        weights,
        out_weights,
        smem=(0,),
        scratch=(pltpu.VMEM((columns_here, HID), F32), pltpu.VMEM((columns_here, channels), F32)),
    )
    return result.reshape(node_rows, node_cols, channels)


def solution(mesh):
    placed = (
        P("elem", "span", None),
        P("elem", "span"),
        P(("elem", "span"), None),
        P(),
        P(),
        P(),
        P(),
        P(),
    )
    return jax.shard_map(
        shards, mesh=mesh, in_specs=placed, out_specs=P("elem", "span", None), check_vma=False
    )
```

```python
import math

import jax
import jax.numpy as jnp
import numpy as np
from jax import lax
from jax.experimental import pallas as pl
from jax.experimental.pallas import tpu as pltpu
from jax.sharding import PartitionSpec as P

NP = 4
NV = 4
HID = 512
LEVELS = 32
LANES = 128
COURANT = 0.05
F32 = jnp.float32
BF16 = jnp.bfloat16
VMEM_LIMIT = 16 << 20


def gll_table():
    nodes = np.array([-1.0, -1.0 / math.sqrt(5.0), 1.0 / math.sqrt(5.0), 1.0])
    width = nodes.shape[0]
    table = np.zeros((width, width))
    for row in range(width):
        for column in range(width):
            if row != column:
                upper = np.prod(
                    [nodes[row] - nodes[other] for other in range(width) if other != row]
                )
                lower = np.prod(
                    [nodes[column] - nodes[other] for other in range(width) if other != column]
                )
                table[row, column] = upper / (lower * (nodes[row] - nodes[column]))
            else:
                table[row, row] = sum(
                    (1.0 / (nodes[row] - nodes[other]) for other in range(width) if other != row)
                )
    return table


D = [[float(v) for v in row] for row in gll_table()]


def winds(f):
    flat = f.reshape(-1, LANES)
    v = lax.broadcasted_iota(jnp.int32, flat.shape, 1) % NV
    one = pltpu.roll(flat, 1, 1)
    two = pltpu.roll(flat, 2, 1)
    three = pltpu.roll(flat, 3, 1)
    back = pltpu.roll(flat, LANES - 1, 1)
    first = jnp.where(v == 0, flat, jnp.where(v == 1, one, jnp.where(v == 2, two, three)))
    second = jnp.where(v == 0, back, jnp.where(v == 1, flat, jnp.where(v == 2, one, two)))
    return first.reshape(f.shape), second.reshape(f.shape)


def along_x(f):
    rows = f.reshape(f.shape[0] // NP, NP, f.shape[1], LANES)
    pieces = []
    for i in range(NP):
        total = D[i][0] * rows[:, 0]
        for k in range(1, NP):
            total = total + D[i][k] * rows[:, k]
        pieces.append(total)
    return jnp.stack(pieces, axis=1).reshape(f.shape)


def along_y(f):
    size = f.shape[1]
    y = lax.broadcasted_iota(jnp.int32, (1, size, LANES), 1) % NP
    total = None
    for shift in range(-(NP - 1), NP):
        factor = jnp.zeros((1, size, LANES), F32)
        for i in range(NP):
            if 0 <= i + shift < NP:
                factor = jnp.where(y == i, D[i][i + shift], factor)
        moved = f if shift == 0 else pltpu.roll(f, (-shift) % size, 1)
        term = factor * moved
        total = term if total is None else total + term
    return total


def average_y(f, left, right):
    size = f.shape[1]
    y = lax.broadcasted_iota(jnp.int32, (1, size, LANES), 1)
    ahead = pltpu.roll(f, size - 1, 1)
    behind = pltpu.roll(f, 1, 1)
    other = jnp.where(y % NP == NP - 1, ahead, jnp.where(y % NP == 0, behind, f))
    other = jnp.where(y == size - 1, right, jnp.where(y == 0, left, other))
    return (f + other) * 0.5


def average_x(f, before, after):
    rows = f.shape[0]
    pieces = []
    for r in range(rows):
        if r % NP == 0:
            other = before if r == 0 else f[r - 1]
            pieces.append((f[r] + other) * 0.5)
        elif r % NP == NP - 1:
            other = after if r == rows - 1 else f[r + 1]
            pieces.append((f[r] + other) * 0.5)
        else:
            pieces.append(f[r])
    return jnp.stack(pieces, axis=0)


def first_kernel(state_ref, surface_ref, moved_ref, to_before_ref, to_after_ref, spread_ref):
    spread_ref[...] = jnp.broadcast_to(surface_ref[...][None], spread_ref.shape)
    f = state_ref[...]
    wind_x, wind_y = winds(f)
    a = f - COURANT * (wind_x * along_x(f) + wind_y * along_y(f))
    moved_ref[...] = a
    n = a.shape[0]
    to_before_ref[0] = a[0]
    to_before_ref[1] = D[0][1] * a[1] + D[0][2] * a[2] + D[0][3] * ((a[3] + a[4]) * 0.5)
    to_after_ref[0] = a[n - 1]
    to_after_ref[1] = (
        D[3][0] * ((a[n - 4] + a[n - 5]) * 0.5) + D[3][1] * a[n - 3] + D[3][2] * a[n - 2]
    )


def second_kernel(moved_ref, before_ref, after_ref, g_ref, to_left_ref, to_right_ref):
    g = average_x(moved_ref[...], before_ref[0], after_ref[0])
    g_ref[...] = g
    rows, size, _ = g.shape
    middle = (g[:, 3] + g[:, 4]) * 0.5
    to_left_ref[0:rows] = g[:, 0]
    to_left_ref[rows : 2 * rows] = D[0][1] * g[:, 1] + D[0][2] * g[:, 2] + D[0][3] * middle
    to_right_ref[0:rows] = g[:, size - 1]
    to_right_ref[rows : 2 * rows] = (
        D[3][0] * middle + D[3][1] * g[:, size - 3] + D[3][2] * g[:, size - 2]
    )
    up, down = before_ref[1], after_ref[1]
    y = lax.broadcasted_iota(jnp.int32, (size, LANES), 0)
    to_left_ref[2 * rows : 2 * rows + 8] = jnp.where(
        y == 0, up, jnp.where(y == 1, pltpu.roll(down, 1, 0), 0.0)
    )
    to_right_ref[2 * rows : 2 * rows + 8] = jnp.where(
        y == 0, pltpu.roll(up, 1, 0), jnp.where(y == 1, pltpu.roll(down, 2, 0), 0.0)
    )


def third_kernel(g_ref, before_ref, after_ref, left_ref, right_ref, field_ref):
    g = g_ref[...]
    rows, size, _ = g.shape
    left_g = left_ref[0:rows].reshape(rows, 1, LANES)
    right_g = right_ref[0:rows].reshape(rows, 1, LANES)
    f = average_y(g, left_g, right_g)
    tail_l = left_ref[2 * rows : 2 * rows + 8]
    tail_r = right_ref[2 * rows : 2 * rows + 8]
    up = average_y(before_ref[1:2], tail_l[0:1].reshape(1, 1, LANES), tail_r[0:1].reshape(1, 1, LANES))[0]
    down = average_y(after_ref[1:2], tail_l[1:2].reshape(1, 1, LANES), tail_r[1:2].reshape(1, 1, LANES))[0]
    slope_x = average_x(
        along_x(f), D[3][3] * f[0] + up, D[0][0] * f[rows - 1] + down
    )
    other_l = left_ref[rows : 2 * rows].reshape(rows, 1, LANES)
    other_r = right_ref[rows : 2 * rows].reshape(rows, 1, LANES)
    slope_y = average_y(along_y(f), D[3][3] * f + other_l, D[0][0] * f + other_r)
    wind_x, wind_y = winds(f)
    field_ref[...] = f - COURANT * (wind_x * slope_x + wind_y * slope_y)


def lstm_kernel(
    slots_ref, core_ref, near_ref, far_ref, field_ref, state_w_ref, surf_w_ref, hidden_w_ref, bias_ref, out_w_ref,
    out_ref, in_w_ref, cell_ref, part_ref, pend_ref, past_ref,
):
    rows = field_ref.shape[0]
    gates = 4 * HID
    unit = HID // 2
    row = lax.broadcasted_iota(jnp.int32, (64, NV), 0)
    col = lax.broadcasted_iota(jnp.int32, (64, NV), 1)
    spread = (row % NV == col).astype(BF16)
    in_w_ref[0:64] = jnp.dot(spread, state_w_ref[...], preferred_element_type=F32).astype(BF16)
    bias = bias_ref[...]
    high = bias.astype(BF16).astype(F32)
    rest = bias - high
    mid = rest.astype(BF16).astype(F32)
    low = rest - mid
    r = lax.broadcasted_iota(jnp.int32, (16, 1), 0)
    parts = jnp.where(r == 0, high, jnp.where(r == 1, mid, jnp.where(r == 2, low, 0.0)))
    in_w_ref[64:80] = parts.astype(BF16)
    in_w_ref[80:96] = surf_w_ref[...]
    in_w_ref[96:128] = jnp.zeros((32, gates), BF16)

    feature_lane = lax.broadcasted_iota(jnp.int32, (16, LANES), 1)
    core = core_ref[0]

    def fetch(c, acc):
        slot = slots_ref[jnp.bitwise_and(c, 7), lax.shift_right_logical(c, 3)]
        owner = lax.shift_right_logical(slot, 8)
        place = jnp.bitwise_and(slot, 255)
        half = pl.multiple_of(jnp.bitwise_and(place, 128), 128)
        index = jnp.bitwise_or(
            lax.shift_left(lax.shift_right_logical(owner, 3), 2), jnp.bitwise_and(owner, 3)
        )
        here = jnp.bitwise_and(lax.shift_right_logical(owner, 2), 1) == core
        near = near_ref[index, :, pl.ds(half, LANES)]
        far = far_ref[index, :, pl.ds(half, LANES)]
        tile = jnp.where(here, near, far).astype(F32)
        shift = jnp.bitwise_and(c - place + 256, 127)
        return jnp.where(feature_lane == c, pltpu.roll(tile, shift, 1), acc)

    surf = lax.fori_loop(0, rows, fetch, jnp.zeros((16, LANES), F32), unroll=8)
    surf = jnp.concatenate(
        [jnp.zeros((80, LANES), F32), surf, jnp.zeros((32, LANES), F32)], axis=0
    ).T
    lane = lax.broadcasted_iota(jnp.int32, (rows, LANES), 1)
    fixed = jnp.where((lane >= 64) & (lane < 67), 0.5, 0.5 * surf)
    field = field_ref[...]
    half_field = 0.5 * field.astype(BF16).astype(F32)
    swapped = pltpu.roll(half_field, 64, 1)

    def level_input(level):
        source = jnp.where(level < LEVELS // 2, half_field, swapped)
        return jnp.where(lane // NV == level % (LEVELS // 2), source, fixed).astype(BF16)

    def dot(a, b):
        return jnp.dot(a, b, preferred_element_type=F32)

    def cols(q, j):
        return slice(q * HID + j * unit, q * HID + (j + 1) * unit)

    def cell_step(g, j, first=False):
        s = slice(j * unit, (j + 1) * unit)
        c = (0.5 * jnp.tanh(g[0]) + 0.5) * jnp.tanh(g[2] + g[2])
        if not first:
            c = c + (0.5 * jnp.tanh(g[1]) + 0.5) * cell_ref[:, s]
        cell_ref[:, s] = c
        return ((0.25 * jnp.tanh(g[3]) + 0.25) * jnp.tanh(c)).astype(BF16)

    x = level_input(0)
    low_half = cell_step([dot(x, in_w_ref[:, cols(q, 0)]) for q in range(4)], 0, True)
    for q in range(4):
        pend_ref[q] = dot(x, in_w_ref[:, cols(q, 1)])
    cell_ref[:, unit:HID] = jnp.zeros((rows, unit), F32)

    def finish(level, low_half):
        high_half = cell_step([pend_ref[q] for q in range(4)], 1)
        past_ref[level] = jnp.concatenate([low_half, high_half], axis=1)
        return high_half

    def step(level, low_half):
        x = level_input(level)
        for j in range(2):
            for q in range(4):
                part_ref[j, q] = dot(x, in_w_ref[:, cols(q, j)]) + dot(
                    low_half, hidden_w_ref[0:unit, cols(q, j)]
                )
        high_half = finish(level - 1, low_half)
        g = [
            part_ref[0, q] + dot(high_half, hidden_w_ref[unit:HID, cols(q, 0)]) for q in range(4)
        ]
        new = cell_step(g, 0)
        for q in range(4):
            pend_ref[q] = part_ref[1, q] + dot(high_half, hidden_w_ref[unit:HID, cols(q, 1)])
        return new

    low_half = lax.fori_loop(1, LEVELS, step, low_half, unroll=4)
    finish(LEVELS - 1, low_half)
    row = lax.broadcasted_iota(jnp.int32, (NV, LANES), 0)
    col = lax.broadcasted_iota(jnp.int32, (NV, LANES), 1)
    spread = (col % NV == row).astype(BF16)
    out_w = lax.dot_general(
        out_w_ref[...], spread, (((0,), (0,)), ((), ())), preferred_element_type=F32
    )
    out_w = (out_w + out_w).astype(BF16)
    group = 8
    gain = jnp.zeros((rows, LANES), F32)
    for k in range(LEVELS // group):
        p = dot(past_ref[k * group : (k + 1) * group].reshape(group * rows, HID), out_w)
        for i in range(group):
            gain = jnp.where(lane // NV == k * group + i, p[i * rows : (i + 1) * rows], gain)
    out_ref[...] = field + gain.astype(BF16).astype(F32)


def call(kernel, out_shape, *args, smem=(), scratch=(), cost=None):
    return pl.pallas_call(
        kernel,
        out_shape=out_shape,
        in_specs=[
            pl.BlockSpec(memory_space=pltpu.SMEM if i in smem else pltpu.VMEM)
            for i in range(len(args))
        ],
        out_specs=jax.tree.map(lambda _: pl.BlockSpec(memory_space=pltpu.VMEM), out_shape),
        scratch_shapes=list(scratch),
        compiler_params=pltpu.CompilerParams(vmem_limit_bytes=VMEM_LIMIT),
        cost_estimate=cost,
    )(*args)


def like(*shape, dtype=F32):
    return jax.ShapeDtypeStruct(shape, dtype)


ALL = ("z", "y", "c", "x")
ELEM = ("z", "y", "c")


def exchange(to_lower, to_upper, axes):
    size = math.prod(lax.axis_size(a) for a in axes)
    up = [(i, (i + 1) % size) for i in range(size)]
    down = [(j, i) for i, j in up]
    return lax.ppermute(to_upper, axes, up), lax.ppermute(to_lower, axes, down)


def shards(state, assignment, surface, w_state, w_surf, w_hidden, bias, w_out):
    node_rows, node_cols, channels = state.shape
    columns_here = node_rows * node_cols
    slot_count, features = surface.shape
    peers = lax.axis_size("z") * lax.axis_size("y") * lax.axis_size("x")
    block = like(node_rows, node_cols, channels)
    edge = like(2, node_cols, channels)
    moved, to_before, to_after, spread = call(
        first_kernel,
        (block, edge, edge, like(peers, features, slot_count, dtype=BF16)),
        state,
        surface.T,
    )
    before, after = exchange(to_before, to_after, ELEM)
    near = lax.all_to_all(spread, ("z", "y", "x"), split_axis=0, concat_axis=0, tiled=True)
    far = lax.ppermute(near, "c", [(0, 1), (1, 0)])
    side = like(2 * node_rows + 8, channels)
    g, to_left, to_right = call(second_kernel, (block, side, side), moved, before, after)
    left, right = exchange(to_left, to_right, ("x",))
    field = call(third_kernel, block, g, before, after, left, right)
    core = lax.axis_index("c").reshape(1)
    result = call(
        lstm_kernel,
        like(columns_here, channels),
        assignment.T,
        core,
        near,
        far,
        field.reshape(columns_here, channels),
        w_state,
        w_surf,
        w_hidden,
        bias.reshape(1, 4 * HID),
        w_out.T,
        smem=(0, 1),
        scratch=(
            pltpu.VMEM((LANES, 4 * HID), BF16),
            pltpu.VMEM((columns_here, HID), F32),
            pltpu.VMEM((2, 4, columns_here, HID // 2), F32),
            pltpu.VMEM((4, columns_here, HID // 2), F32),
            pltpu.VMEM((LEVELS, columns_here, HID), BF16),
        ),
    )
    return result.reshape(node_rows, node_cols, channels)


def solution(mesh):
    devices = mesh.devices
    mesh = jax.sharding.Mesh(devices.reshape(4, 4, 2, 4), ALL)
    placed = (
        P(ELEM, "x", None),
        P(ELEM, "x"),
        P(ALL, None),
        P(),
        P(),
        P(),
        P(),
        P(),
    )
    return jax.shard_map(
        shards, mesh=mesh, in_specs=placed, out_specs=P(ELEM, "x", None), check_vma=False
    )
```

```python
import math

import jax
import jax.numpy as jnp
import numpy as np
from jax import lax
from jax.experimental import pallas as pl
from jax.experimental.pallas import tpu as pltpu
from jax.sharding import PartitionSpec as P

NP = 4
NV = 4
HID = 512
LEVELS = 32
LANES = 128
COURANT = 0.05
F32 = jnp.float32
BF16 = jnp.bfloat16
VMEM_LIMIT = 16 << 20


def gll_table():
    nodes = np.array([-1.0, -1.0 / math.sqrt(5.0), 1.0 / math.sqrt(5.0), 1.0])
    width = nodes.shape[0]
    table = np.zeros((width, width))
    for row in range(width):
        for column in range(width):
            if row != column:
                upper = np.prod(
                    [nodes[row] - nodes[other] for other in range(width) if other != row]
                )
                lower = np.prod(
                    [nodes[column] - nodes[other] for other in range(width) if other != column]
                )
                table[row, column] = upper / (lower * (nodes[row] - nodes[column]))
            else:
                table[row, row] = sum(
                    (1.0 / (nodes[row] - nodes[other]) for other in range(width) if other != row)
                )
    return table


D = [[float(v) for v in row] for row in gll_table()]


def winds(f):
    flat = f.reshape(-1, LANES)
    v = lax.broadcasted_iota(jnp.int32, flat.shape, 1) % NV
    one = pltpu.roll(flat, 1, 1)
    two = pltpu.roll(flat, 2, 1)
    three = pltpu.roll(flat, 3, 1)
    back = pltpu.roll(flat, LANES - 1, 1)
    first = jnp.where(v == 0, flat, jnp.where(v == 1, one, jnp.where(v == 2, two, three)))
    second = jnp.where(v == 0, back, jnp.where(v == 1, flat, jnp.where(v == 2, one, two)))
    return first.reshape(f.shape), second.reshape(f.shape)


def along_x(f):
    rows = f.reshape(f.shape[0] // NP, NP, f.shape[1], LANES)
    pieces = []
    for i in range(NP):
        total = D[i][0] * rows[:, 0]
        for k in range(1, NP):
            total = total + D[i][k] * rows[:, k]
        pieces.append(total)
    return jnp.stack(pieces, axis=1).reshape(f.shape)


def along_y(f):
    size = f.shape[1]
    y = lax.broadcasted_iota(jnp.int32, (1, size, LANES), 1) % NP
    total = None
    for shift in range(-(NP - 1), NP):
        factor = jnp.zeros((1, size, LANES), F32)
        for i in range(NP):
            if 0 <= i + shift < NP:
                factor = jnp.where(y == i, D[i][i + shift], factor)
        moved = f if shift == 0 else pltpu.roll(f, (-shift) % size, 1)
        term = factor * moved
        total = term if total is None else total + term
    return total


def average_y(f, left, right):
    size = f.shape[1]
    y = lax.broadcasted_iota(jnp.int32, (1, size, LANES), 1)
    ahead = pltpu.roll(f, size - 1, 1)
    behind = pltpu.roll(f, 1, 1)
    other = jnp.where(y % NP == NP - 1, ahead, jnp.where(y % NP == 0, behind, f))
    other = jnp.where(y == size - 1, right, jnp.where(y == 0, left, other))
    return (f + other) * 0.5


def average_x(f, before, after):
    rows = f.shape[0]
    pieces = []
    for r in range(rows):
        if r % NP == 0:
            other = before if r == 0 else f[r - 1]
            pieces.append((f[r] + other) * 0.5)
        elif r % NP == NP - 1:
            other = after if r == rows - 1 else f[r + 1]
            pieces.append((f[r] + other) * 0.5)
        else:
            pieces.append(f[r])
    return jnp.stack(pieces, axis=0)


def spread_kernel(surface_ref, spread_ref, here_ref, arrived):
    copy = pltpu.make_async_copy(surface_ref, here_ref, arrived)
    copy.start()
    copy.wait()
    spread_ref[...] = jnp.broadcast_to(here_ref[...][None], spread_ref.shape)


def first_kernel(state_ref, moved_ref, to_before_ref, to_after_ref, here_ref, arrived):
    copy = pltpu.make_async_copy(state_ref, here_ref, arrived)
    copy.start()
    copy.wait()
    f = here_ref[...]
    wind_x, wind_y = winds(f)
    a = f - COURANT * (wind_x * along_x(f) + wind_y * along_y(f))
    moved_ref[...] = a
    n = a.shape[0]
    to_before_ref[0] = a[0]
    to_before_ref[1] = D[0][1] * a[1] + D[0][2] * a[2] + D[0][3] * ((a[3] + a[4]) * 0.5)
    to_after_ref[0] = a[n - 1]
    to_after_ref[1] = (
        D[3][0] * ((a[n - 4] + a[n - 5]) * 0.5) + D[3][1] * a[n - 3] + D[3][2] * a[n - 2]
    )


def second_kernel(moved_ref, before_ref, after_ref, g_ref, to_left_ref, to_right_ref):
    g = average_x(moved_ref[...], before_ref[0], after_ref[0])
    g_ref[...] = g
    rows, size, _ = g.shape
    middle = (g[:, 3] + g[:, 4]) * 0.5
    to_left_ref[0:rows] = g[:, 0]
    to_left_ref[rows : 2 * rows] = D[0][1] * g[:, 1] + D[0][2] * g[:, 2] + D[0][3] * middle
    to_right_ref[0:rows] = g[:, size - 1]
    to_right_ref[rows : 2 * rows] = (
        D[3][0] * middle + D[3][1] * g[:, size - 3] + D[3][2] * g[:, size - 2]
    )
    up, down = before_ref[1], after_ref[1]
    y = lax.broadcasted_iota(jnp.int32, (size, LANES), 0)
    to_left_ref[2 * rows : 2 * rows + 8] = jnp.where(
        y == 0, up, jnp.where(y == 1, pltpu.roll(down, 1, 0), 0.0)
    )
    to_right_ref[2 * rows : 2 * rows + 8] = jnp.where(
        y == 0, pltpu.roll(up, 1, 0), jnp.where(y == 1, pltpu.roll(down, 2, 0), 0.0)
    )


def third_kernel(g_ref, before_ref, after_ref, left_ref, right_ref, field_ref):
    g = g_ref[...]
    rows, size, _ = g.shape
    left_g = left_ref[0:rows].reshape(rows, 1, LANES)
    right_g = right_ref[0:rows].reshape(rows, 1, LANES)
    f = average_y(g, left_g, right_g)
    tail_l = left_ref[2 * rows : 2 * rows + 8]
    tail_r = right_ref[2 * rows : 2 * rows + 8]
    up = average_y(before_ref[1:2], tail_l[0:1].reshape(1, 1, LANES), tail_r[0:1].reshape(1, 1, LANES))[0]
    down = average_y(after_ref[1:2], tail_l[1:2].reshape(1, 1, LANES), tail_r[1:2].reshape(1, 1, LANES))[0]
    slope_x = average_x(
        along_x(f), D[3][3] * f[0] + up, D[0][0] * f[rows - 1] + down
    )
    other_l = left_ref[rows : 2 * rows].reshape(rows, 1, LANES)
    other_r = right_ref[rows : 2 * rows].reshape(rows, 1, LANES)
    slope_y = average_y(along_y(f), D[3][3] * f + other_l, D[0][0] * f + other_r)
    wind_x, wind_y = winds(f)
    field_ref[...] = f - COURANT * (wind_x * slope_x + wind_y * slope_y)


def lstm_kernel(
    near_ref, far_ref, field_ref, *refs
):
    kept, out_ref = refs[:6], refs[6]
    slots_ref, state_w_ref, surf_w_ref, hidden_w_ref, bias_ref, out_w_ref = refs[7:13]
    in_w_ref, cell_ref, part_ref, pend_ref, past_ref, arrived = refs[13:]
    copies = [
        pltpu.make_async_copy(source, target, arrived.at[i])
        for i, (source, target) in enumerate(zip(kept, refs[7:13]))
    ]
    for copy in copies:
        copy.start()
    rows = field_ref.shape[0]
    gates = 4 * HID
    unit = HID // 2
    for i in (1, 2, 4):
        copies[i].wait()
    row = lax.broadcasted_iota(jnp.int32, (64, NV), 0)
    col = lax.broadcasted_iota(jnp.int32, (64, NV), 1)
    spread = (row % NV == col).astype(BF16)
    in_w_ref[0:64] = jnp.dot(spread, state_w_ref[...], preferred_element_type=F32).astype(BF16)
    bias = bias_ref[...]
    high = bias.astype(BF16).astype(F32)
    rest = bias - high
    mid = rest.astype(BF16).astype(F32)
    low = rest - mid
    r = lax.broadcasted_iota(jnp.int32, (16, 1), 0)
    parts = jnp.where(r == 0, high, jnp.where(r == 1, mid, jnp.where(r == 2, low, 0.0)))
    in_w_ref[64:80] = parts.astype(BF16)
    in_w_ref[80:96] = surf_w_ref[...]
    in_w_ref[96:128] = jnp.zeros((32, gates), BF16)

    feature_lane = lax.broadcasted_iota(jnp.int32, (16, LANES), 1)
    core = jnp.bitwise_and(lax.axis_index("c"), 1)
    copies[0].wait()

    def fetch(c, acc):
        slot = slots_ref[jnp.bitwise_and(c, 7), lax.shift_right_logical(c, 3)]
        owner = lax.shift_right_logical(slot, 8)
        place = jnp.bitwise_and(slot, 255)
        half = pl.multiple_of(jnp.bitwise_and(place, 128), 128)
        index = jnp.bitwise_or(
            lax.shift_left(lax.shift_right_logical(owner, 3), 2), jnp.bitwise_and(owner, 3)
        )
        here = jnp.bitwise_and(lax.shift_right_logical(owner, 2), 1) == core
        near = near_ref[index, :, pl.ds(half, LANES)]
        far = far_ref[index, :, pl.ds(half, LANES)]
        tile = jnp.where(here, near, far).astype(F32)
        shift = jnp.bitwise_and(c - place + 256, 127)
        return jnp.where(feature_lane == c, pltpu.roll(tile, shift, 1), acc)

    surf = lax.fori_loop(0, rows, fetch, jnp.zeros((16, LANES), F32), unroll=8)
    surf = jnp.concatenate(
        [jnp.zeros((80, LANES), F32), surf, jnp.zeros((32, LANES), F32)], axis=0
    ).T
    lane = lax.broadcasted_iota(jnp.int32, (rows, LANES), 1)
    fixed = jnp.where((lane >= 64) & (lane < 67), 0.5, 0.5 * surf)
    field = field_ref[...]
    half_field = 0.5 * field.astype(BF16).astype(F32)
    swapped = pltpu.roll(half_field, 64, 1)

    def level_input(level):
        source = jnp.where(level < LEVELS // 2, half_field, swapped)
        return jnp.where(lane // NV == level % (LEVELS // 2), source, fixed).astype(BF16)

    def dot(a, b):
        return jnp.dot(a, b, preferred_element_type=F32)

    def cols(q, j):
        return slice(q * HID + j * unit, q * HID + (j + 1) * unit)

    def cell_step(g, j, first=False):
        s = slice(j * unit, (j + 1) * unit)
        c = (0.5 * jnp.tanh(g[0]) + 0.5) * jnp.tanh(g[2] + g[2])
        if not first:
            c = c + (0.5 * jnp.tanh(g[1]) + 0.5) * cell_ref[:, s]
        cell_ref[:, s] = c
        return ((0.25 * jnp.tanh(g[3]) + 0.25) * jnp.tanh(c)).astype(BF16)

    x = level_input(0)
    low_half = cell_step([dot(x, in_w_ref[:, cols(q, 0)]) for q in range(4)], 0, True)
    for q in range(4):
        pend_ref[q] = dot(x, in_w_ref[:, cols(q, 1)])
    cell_ref[:, unit:HID] = jnp.zeros((rows, unit), F32)

    def finish(level, low_half):
        high_half = cell_step([pend_ref[q] for q in range(4)], 1)
        past_ref[level] = jnp.concatenate([low_half, high_half], axis=1)
        return high_half

    def step(level, low_half):
        x = level_input(level)
        for j in range(2):
            for q in range(4):
                part_ref[j, q] = dot(x, in_w_ref[:, cols(q, j)]) + dot(
                    low_half, hidden_w_ref[0:unit, cols(q, j)]
                )
        high_half = finish(level - 1, low_half)
        g = [
            part_ref[0, q] + dot(high_half, hidden_w_ref[unit:HID, cols(q, 0)]) for q in range(4)
        ]
        new = cell_step(g, 0)
        for q in range(4):
            pend_ref[q] = part_ref[1, q] + dot(high_half, hidden_w_ref[unit:HID, cols(q, 1)])
        return new

    copies[3].wait()
    low_half = lax.fori_loop(1, LEVELS, step, low_half, unroll=4)
    finish(LEVELS - 1, low_half)
    copies[5].wait()
    row = lax.broadcasted_iota(jnp.int32, (NV, LANES), 0)
    col = lax.broadcasted_iota(jnp.int32, (NV, LANES), 1)
    spread = (col % NV == row).astype(BF16)
    out_w = lax.dot_general(
        out_w_ref[...], spread, (((0,), (0,)), ((), ())), preferred_element_type=F32
    )
    out_w = (out_w + out_w).astype(BF16)
    group = 8
    gain = jnp.zeros((rows, LANES), F32)
    for k in range(LEVELS // group):
        p = dot(past_ref[k * group : (k + 1) * group].reshape(group * rows, HID), out_w)
        for i in range(group):
            gain = jnp.where(lane // NV == k * group + i, p[i * rows : (i + 1) * rows], gain)
    out_ref[...] = field + gain.astype(BF16).astype(F32)


def call(kernel, out_shape, *args, kept=(), scratch=(), cost=None):
    placed = len(args)
    args = (*args, *[pltpu.with_memory_space_constraint(a, pltpu.HBM) for a in kept])
    return pl.pallas_call(
        kernel,
        out_shape=out_shape,
        in_specs=[
            pl.BlockSpec(memory_space=pltpu.VMEM if i < placed else pltpu.HBM)
            for i in range(len(args))
        ],
        out_specs=jax.tree.map(lambda _: pl.BlockSpec(memory_space=pltpu.VMEM), out_shape),
        scratch_shapes=list(scratch),
        compiler_params=pltpu.CompilerParams(vmem_limit_bytes=VMEM_LIMIT),
        cost_estimate=cost,
    )(*args)


def like(*shape, dtype=F32):
    return jax.ShapeDtypeStruct(shape, dtype)


ALL = ("z", "y", "c", "x")
ELEM = ("z", "y", "c")


def exchange(to_lower, to_upper, axes):
    size = math.prod(lax.axis_size(a) for a in axes)
    up = [(i, (i + 1) % size) for i in range(size)]
    down = [(j, i) for i, j in up]
    return lax.ppermute(to_upper, axes, up), lax.ppermute(to_lower, axes, down)


def shards(state, assignment, surface, w_state, w_surf, w_hidden, bias, w_out):
    node_rows, node_cols, channels = state.shape
    columns_here = node_rows * node_cols
    slot_count, features = surface.shape
    peers = lax.axis_size("z") * lax.axis_size("y") * lax.axis_size("x")
    block = like(node_rows, node_cols, channels)
    edge = like(2, node_cols, channels)
    spread = call(
        spread_kernel,
        like(peers, features, slot_count, dtype=BF16),
        kept=(surface.T,),
        scratch=(pltpu.VMEM((features, slot_count), BF16), pltpu.SemaphoreType.DMA(())),
    )
    moved, to_before, to_after = call(
        first_kernel,
        (block, edge, edge),
        kept=(state,),
        scratch=(pltpu.VMEM(state.shape, F32), pltpu.SemaphoreType.DMA(())),
    )
    before, after = exchange(to_before, to_after, ELEM)
    near = lax.all_to_all(spread, ("z", "y", "x"), split_axis=0, concat_axis=0, tiled=True)
    side = like(2 * node_rows + 8, channels)
    g, to_left, to_right = call(second_kernel, (block, side, side), moved, before, after)
    left, right = exchange(to_left, to_right, ("x",))
    field = call(third_kernel, block, g, before, after, left, right)
    near, _ = lax.optimization_barrier((near, field))
    far = lax.ppermute(near, "c", [(0, 1), (1, 0)])
    kept = (assignment.T, w_state, w_surf, w_hidden, bias.reshape(1, 4 * HID), w_out.T)
    result = call(
        lstm_kernel,
        like(columns_here, channels),
        near,
        far,
        field.reshape(columns_here, channels),
        kept=kept,
        scratch=(
            pltpu.SMEM(kept[0].shape, kept[0].dtype),
            *[pltpu.VMEM(a.shape, a.dtype) for a in kept[1:]],
            pltpu.VMEM((LANES, 4 * HID), BF16),
            pltpu.VMEM((columns_here, HID), F32),
            pltpu.VMEM((2, 4, columns_here, HID // 2), F32),
            pltpu.VMEM((4, columns_here, HID // 2), F32),
            pltpu.VMEM((LEVELS, columns_here, HID), BF16),
            pltpu.SemaphoreType.DMA((len(kept),)),
        ),
    )
    return result.reshape(node_rows, node_cols, channels)


def solution(mesh):
    devices = mesh.devices
    mesh = jax.sharding.Mesh(devices.reshape(4, 4, 2, 4), ALL)
    placed = (
        P(ELEM, "x", None),
        P(ELEM, "x"),
        P(ALL, None),
        P(),
        P(),
        P(),
        P(),
        P(),
    )
    return jax.shard_map(
        shards, mesh=mesh, in_specs=placed, out_specs=P(ELEM, "x", None), check_vma=False
    )
```

```python
import math

import jax
import jax.numpy as jnp
import numpy as np
from jax import lax
from jax.experimental import pallas as pl
from jax.experimental.pallas import tpu as pltpu
from jax.sharding import PartitionSpec as P

NP = 4
NV = 4
HID = 512
LEVELS = 32
LANES = 128
COURANT = 0.05
F32 = jnp.float32
BF16 = jnp.bfloat16
UNR = 15
VMEM_LIMIT = 16 << 20


def gll_table():
    nodes = np.array([-1.0, -1.0 / math.sqrt(5.0), 1.0 / math.sqrt(5.0), 1.0])
    width = nodes.shape[0]
    table = np.zeros((width, width))
    for row in range(width):
        for column in range(width):
            if row != column:
                upper = np.prod(
                    [nodes[row] - nodes[other] for other in range(width) if other != row]
                )
                lower = np.prod(
                    [nodes[column] - nodes[other] for other in range(width) if other != column]
                )
                table[row, column] = upper / (lower * (nodes[row] - nodes[column]))
            else:
                table[row, row] = sum(
                    (1.0 / (nodes[row] - nodes[other]) for other in range(width) if other != row)
                )
    return table


D = [[float(v) for v in row] for row in gll_table()]


def winds(f):
    flat = f.reshape(-1, LANES)
    v = lax.broadcasted_iota(jnp.int32, flat.shape, 1) % NV
    one = pltpu.roll(flat, 1, 1)
    two = pltpu.roll(flat, 2, 1)
    three = pltpu.roll(flat, 3, 1)
    back = pltpu.roll(flat, LANES - 1, 1)
    first = jnp.where(v == 0, flat, jnp.where(v == 1, one, jnp.where(v == 2, two, three)))
    second = jnp.where(v == 0, back, jnp.where(v == 1, flat, jnp.where(v == 2, one, two)))
    return first.reshape(f.shape), second.reshape(f.shape)


def along_x(f):
    rows = f.reshape(f.shape[0] // NP, NP, f.shape[1], LANES)
    pieces = []
    for i in range(NP):
        total = D[i][0] * rows[:, 0]
        for k in range(1, NP):
            total = total + D[i][k] * rows[:, k]
        pieces.append(total)
    return jnp.stack(pieces, axis=1).reshape(f.shape)


def along_y(f):
    size = f.shape[1]
    y = lax.broadcasted_iota(jnp.int32, (1, size, LANES), 1) % NP
    total = None
    for shift in range(-(NP - 1), NP):
        factor = jnp.zeros((1, size, LANES), F32)
        for i in range(NP):
            if 0 <= i + shift < NP:
                factor = jnp.where(y == i, D[i][i + shift], factor)
        moved = f if shift == 0 else pltpu.roll(f, (-shift) % size, 1)
        term = factor * moved
        total = term if total is None else total + term
    return total


def average_y(f, left, right):
    size = f.shape[1]
    y = lax.broadcasted_iota(jnp.int32, (1, size, LANES), 1)
    ahead = pltpu.roll(f, size - 1, 1)
    behind = pltpu.roll(f, 1, 1)
    other = jnp.where(y % NP == NP - 1, ahead, jnp.where(y % NP == 0, behind, f))
    other = jnp.where(y == size - 1, right, jnp.where(y == 0, left, other))
    return (f + other) * 0.5


def average_x(f, before, after):
    rows = f.shape[0]
    pieces = []
    for r in range(rows):
        if r % NP == 0:
            other = before if r == 0 else f[r - 1]
            pieces.append((f[r] + other) * 0.5)
        elif r % NP == NP - 1:
            other = after if r == rows - 1 else f[r + 1]
            pieces.append((f[r] + other) * 0.5)
        else:
            pieces.append(f[r])
    return jnp.stack(pieces, axis=0)


def spread_kernel(surface_ref, spread_ref, here_ref, arrived):
    copy = pltpu.make_async_copy(surface_ref, here_ref, arrived)
    copy.start()
    copy.wait()
    spread_ref[...] = jnp.broadcast_to(here_ref[...][None], spread_ref.shape)


def first_kernel(state_ref, moved_ref, to_before_ref, to_after_ref, here_ref, arrived):
    copy = pltpu.make_async_copy(state_ref, here_ref, arrived)
    copy.start()
    copy.wait()
    f = here_ref[...]
    wind_x, wind_y = winds(f)
    a = f - COURANT * (wind_x * along_x(f) + wind_y * along_y(f))
    moved_ref[...] = a
    n = a.shape[0]
    to_before_ref[0] = a[0]
    to_before_ref[1] = D[0][1] * a[1] + D[0][2] * a[2] + D[0][3] * ((a[3] + a[4]) * 0.5)
    to_after_ref[0] = a[n - 1]
    to_after_ref[1] = (
        D[3][0] * ((a[n - 4] + a[n - 5]) * 0.5) + D[3][1] * a[n - 3] + D[3][2] * a[n - 2]
    )


def second_kernel(moved_ref, before_ref, after_ref, g_ref, to_left_ref, to_right_ref):
    g = average_x(moved_ref[...], before_ref[0], after_ref[0])
    g_ref[...] = g
    rows, size, _ = g.shape
    middle = (g[:, 3] + g[:, 4]) * 0.5
    to_left_ref[0:rows] = g[:, 0]
    to_left_ref[rows : 2 * rows] = D[0][1] * g[:, 1] + D[0][2] * g[:, 2] + D[0][3] * middle
    to_right_ref[0:rows] = g[:, size - 1]
    to_right_ref[rows : 2 * rows] = (
        D[3][0] * middle + D[3][1] * g[:, size - 3] + D[3][2] * g[:, size - 2]
    )
    up, down = before_ref[1], after_ref[1]
    y = lax.broadcasted_iota(jnp.int32, (size, LANES), 0)
    to_left_ref[2 * rows : 2 * rows + 8] = jnp.where(
        y == 0, up, jnp.where(y == 1, pltpu.roll(down, 1, 0), 0.0)
    )
    to_right_ref[2 * rows : 2 * rows + 8] = jnp.where(
        y == 0, pltpu.roll(up, 1, 0), jnp.where(y == 1, pltpu.roll(down, 2, 0), 0.0)
    )


def third_kernel(g_ref, before_ref, after_ref, left_ref, right_ref, field_ref):
    g = g_ref[...]
    rows, size, _ = g.shape
    left_g = left_ref[0:rows].reshape(rows, 1, LANES)
    right_g = right_ref[0:rows].reshape(rows, 1, LANES)
    f = average_y(g, left_g, right_g)
    tail_l = left_ref[2 * rows : 2 * rows + 8]
    tail_r = right_ref[2 * rows : 2 * rows + 8]
    up = average_y(before_ref[1:2], tail_l[0:1].reshape(1, 1, LANES), tail_r[0:1].reshape(1, 1, LANES))[0]
    down = average_y(after_ref[1:2], tail_l[1:2].reshape(1, 1, LANES), tail_r[1:2].reshape(1, 1, LANES))[0]
    slope_x = average_x(
        along_x(f), D[3][3] * f[0] + up, D[0][0] * f[rows - 1] + down
    )
    other_l = left_ref[rows : 2 * rows].reshape(rows, 1, LANES)
    other_r = right_ref[rows : 2 * rows].reshape(rows, 1, LANES)
    slope_y = average_y(along_y(f), D[3][3] * f + other_l, D[0][0] * f + other_r)
    wind_x, wind_y = winds(f)
    field_ref[...] = f - COURANT * (wind_x * slope_x + wind_y * slope_y)


def pick_owner(table_ref, pick, wanted, surf):
    peers, features, slot_count = table_ref.shape
    lane = lax.broadcasted_iota(jnp.int32, surf.shape, 1)
    for k in range(0, peers, 16):
        found = lax.dot_general(
            pick,
            table_ref[k : k + 16].reshape(16 * features, slot_count),
            (((1,), (1,)), ((), ())),
            preferred_element_type=F32,
        )
        for half in range(2):
            own = wanted == lane // features + (k + 8 * half)
            surf = jnp.where(own, found[:, half * LANES : (half + 1) * LANES], surf)
    return surf


def prepare_kernel(
    near_ref, slots_hbm, state_w_hbm, surf_w_hbm, hidden_w_hbm, bias_hbm,
    hidden_w_ref, in_w_ref, surf_ref, pick_ref, wanted_ref,
    slots_ref, state_w_ref, surf_w_ref, bias_ref, arrived,
):
    pairs = (
        (slots_hbm, slots_ref),
        (state_w_hbm, state_w_ref),
        (surf_w_hbm, surf_w_ref),
        (bias_hbm, bias_ref),
        (hidden_w_hbm, hidden_w_ref),
    )
    copies = [pltpu.make_async_copy(a, b, arrived.at[i]) for i, (a, b) in enumerate(pairs)]
    for copy in copies:
        copy.start()
    rows = surf_ref.shape[0]
    copies[0].wait()
    slots = slots_ref[...]
    slots = jnp.concatenate(
        [jnp.broadcast_to(slots[:, x : x + 1], (8, 2 * LANES)) for x in range(rows // 8)], axis=0
    )
    place = jnp.bitwise_and(slots, 255)
    owner = lax.shift_right_logical(slots[:, :LANES], 8)
    index = jnp.bitwise_or(
        lax.shift_left(lax.shift_right_logical(owner, 3), 2), jnp.bitwise_and(owner, 3)
    )
    here = jnp.bitwise_and(lax.shift_right_logical(owner, 2), 1) == lax.axis_index("c")
    pick = (lax.broadcasted_iota(jnp.int32, place.shape, 1) == place).astype(BF16)
    pick_ref[...] = pick
    wanted_ref[...] = jnp.where(here, -1, index)
    surf_ref[...] = pick_owner(
        near_ref, pick, jnp.where(here, index, -1), jnp.zeros((rows, LANES), F32)
    )
    for copy in copies[1:4]:
        copy.wait()
    row = lax.broadcasted_iota(jnp.int32, (64, NV), 0)
    col = lax.broadcasted_iota(jnp.int32, (64, NV), 1)
    spread = (row % NV == col).astype(BF16)
    in_w_ref[0:64] = jnp.dot(spread, state_w_ref[...], preferred_element_type=F32).astype(BF16)
    bias = bias_ref[...]
    high = bias.astype(BF16).astype(F32)
    rest = bias - high
    mid = rest.astype(BF16).astype(F32)
    low = rest - mid
    r = lax.broadcasted_iota(jnp.int32, (16, 1), 0)
    parts = jnp.where(r == 0, high, jnp.where(r == 1, mid, jnp.where(r == 2, low, 0.0)))
    in_w_ref[64:80] = parts.astype(BF16)
    in_w_ref[80:96] = surf_w_ref[...]
    in_w_ref[96:128] = jnp.zeros((32, 4 * HID), BF16)
    copies[4].wait()


def lstm_kernel(
    far_ref, field_ref, hidden_w_ref, in_w_ref, surf_ref, pick_ref, wanted_ref, out_w_hbm,
    out_ref, out_w_ref, cell_ref, part_ref, pend_ref, past_ref, feed_ref, arrived,
):
    copy = pltpu.make_async_copy(out_w_hbm, out_w_ref, arrived)
    copy.start()
    rows = field_ref.shape[0]
    features = far_ref.shape[1]
    unit = HID // 2
    surf = pick_owner(far_ref, pick_ref[...], wanted_ref[...], surf_ref[...])
    row = lax.broadcasted_iota(jnp.int32, (LANES, LANES), 0)
    col = lax.broadcasted_iota(jnp.int32, (LANES, LANES), 1)
    fold = (col - 80 == row % features).astype(BF16)
    surf = jnp.dot(surf.astype(BF16), fold, preferred_element_type=F32)
    lane = lax.broadcasted_iota(jnp.int32, (rows, LANES), 1)
    fixed = jnp.where((lane >= 64) & (lane < 67), 0.5, 0.5 * surf)
    field = field_ref[...]
    half_field = 0.5 * field.astype(BF16).astype(F32)
    swapped = pltpu.roll(half_field, 64, 1)

    def level_input(level):
        source = jnp.where(level < LEVELS // 2, half_field, swapped)
        return jnp.where(lane // NV == level % (LEVELS // 2), source, fixed).astype(BF16)

    def dot(a, b):
        return jnp.dot(a, b, preferred_element_type=F32)

    def cols(q, j):
        return slice(q * HID + j * unit, q * HID + (j + 1) * unit)

    def cell_step(g, j, first=False):
        s = slice(j * unit, (j + 1) * unit)
        c = (0.5 * jnp.tanh(g[0]) + 0.5) * jnp.tanh(g[2] + g[2])
        if not first:
            c = c + (0.5 * jnp.tanh(g[1]) + 0.5) * cell_ref[:, s]
        cell_ref[:, s] = c
        return ((0.25 * jnp.tanh(g[3]) + 0.25) * jnp.tanh(c)).astype(BF16)

    x = level_input(0)
    low_half = cell_step([dot(x, in_w_ref[:, cols(q, 0)]) for q in range(4)], 0, True)
    for q in range(4):
        pend_ref[q] = dot(x, in_w_ref[:, cols(q, 1)])
    cell_ref[:, unit:HID] = jnp.zeros((rows, unit), F32)

    def finish(level, low_half):
        high_half = cell_step([pend_ref[q] for q in range(4)], 1)
        past_ref[level] = jnp.concatenate([low_half, high_half], axis=1)
        return high_half

    def feed(level):
        x = jnp.concatenate([level_input(level), level_input(level + 1)], axis=0)
        for j in range(2):
            for q in range(4):
                feed_ref[j, q] = dot(x, in_w_ref[:, cols(q, j)])

    def two_steps(pair, low_half):
        level = 2 * pair + 1
        feed(level)
        return step(level + 1, 1, step(level, 0, low_half))

    def step(level, odd, low_half):
        for j in range(2):
            for q in range(4):
                part_ref[j, q] = feed_ref[j, q, odd * rows : (odd + 1) * rows] + dot(
                    low_half, hidden_w_ref[0:unit, cols(q, j)]
                )
        high_half = finish(level - 1, low_half)
        g = [
            part_ref[0, q] + dot(high_half, hidden_w_ref[unit:HID, cols(q, 0)]) for q in range(4)
        ]
        new = cell_step(g, 0)
        for q in range(4):
            pend_ref[q] = part_ref[1, q] + dot(high_half, hidden_w_ref[unit:HID, cols(q, 1)])
        return new

    low_half = lax.fori_loop(0, LEVELS // 2 - 1, two_steps, low_half, unroll=UNR)
    feed(LEVELS - 1)
    low_half = step(LEVELS - 1, 0, low_half)
    finish(LEVELS - 1, low_half)
    copy.wait()
    out_w = out_w_ref[...].astype(F32)
    out_w = jnp.concatenate([out_w + out_w, jnp.zeros((4, HID), F32)], axis=0).astype(BF16)
    gain = []
    for k in range(0, LEVELS, 8):
        p = lax.dot_general(
            out_w,
            past_ref[k : k + 8].reshape(8 * rows, HID),
            (((1,), (1,)), ((), ())),
            preferred_element_type=F32,
        )
        gain += [p[0:NV, i * rows : (i + 1) * rows] for i in range(8)]
    gain = jnp.concatenate(gain, axis=0).T
    out_ref[...] = field + gain.astype(BF16).astype(F32)


def call(kernel, out_shape, *args, kept=(), scratch=(), cost=None):
    placed = len(args)
    args = (*args, *[pltpu.with_memory_space_constraint(a, pltpu.HBM) for a in kept])
    return pl.pallas_call(
        kernel,
        out_shape=out_shape,
        in_specs=[
            pl.BlockSpec(memory_space=pltpu.VMEM if i < placed else pltpu.HBM)
            for i in range(len(args))
        ],
        out_specs=jax.tree.map(lambda _: pl.BlockSpec(memory_space=pltpu.VMEM), out_shape),
        scratch_shapes=list(scratch),
        compiler_params=pltpu.CompilerParams(vmem_limit_bytes=VMEM_LIMIT),
        cost_estimate=cost,
    )(*args)


def like(*shape, dtype=F32):
    return jax.ShapeDtypeStruct(shape, dtype)


ALL = ("z", "y", "c", "x")
ELEM = ("z", "y", "c")


def exchange(to_lower, to_upper, axes):
    size = math.prod(lax.axis_size(a) for a in axes)
    up = [(i, (i + 1) % size) for i in range(size)]
    down = [(j, i) for i, j in up]
    return lax.ppermute(to_upper, axes, up), lax.ppermute(to_lower, axes, down)


def shards(state, assignment, surface, w_state, w_surf, w_hidden, bias, w_out):
    node_rows, node_cols, channels = state.shape
    columns_here = node_rows * node_cols
    slot_count, features = surface.shape
    peers = lax.axis_size("z") * lax.axis_size("y") * lax.axis_size("x")
    block = like(node_rows, node_cols, channels)
    edge = like(2, node_cols, channels)
    spread = call(
        spread_kernel,
        like(peers, features, slot_count, dtype=BF16),
        kept=(surface.T,),
        scratch=(pltpu.VMEM((features, slot_count), BF16), pltpu.SemaphoreType.DMA(())),
    )
    moved, to_before, to_after = call(
        first_kernel,
        (block, edge, edge),
        kept=(state,),
        scratch=(pltpu.VMEM(state.shape, F32), pltpu.SemaphoreType.DMA(())),
    )
    before, after = exchange(to_before, to_after, ELEM)
    near = lax.all_to_all(spread, ("z", "y", "x"), split_axis=0, concat_axis=0, tiled=True)
    side = like(2 * node_rows + 8, channels)
    g, to_left, to_right = call(second_kernel, (block, side, side), moved, before, after)
    left, right = exchange(to_left, to_right, ("x",))
    field = call(third_kernel, block, g, before, after, left, right)
    near, _ = lax.optimization_barrier((near, field))
    far = lax.ppermute(near, "c", [(0, 1), (1, 0)])
    kept = (assignment.T, w_state, w_surf, w_hidden, bias.reshape(1, 4 * HID))
    prepared = call(
        prepare_kernel,
        (
            like(HID, 4 * HID, dtype=BF16),
            like(LANES, 4 * HID, dtype=BF16),
            like(columns_here, LANES),
            like(columns_here, slot_count, dtype=BF16),
            like(columns_here, LANES, dtype=jnp.int32),
        ),
        near,
        kept=kept,
        scratch=(
            *[pltpu.VMEM(a.shape, a.dtype) for i, a in enumerate(kept) if i != 3],
            pltpu.SemaphoreType.DMA((len(kept),)),
        ),
        cost=pl.CostEstimate(flops=1 << 28, bytes_accessed=4 << 20, transcendentals=0),
    )
    result = call(
        lstm_kernel,
        like(columns_here, channels),
        far,
        field.reshape(columns_here, channels),
        *prepared,
        kept=(w_out.T,),
        scratch=(
            pltpu.VMEM((NV, HID), BF16),
            pltpu.VMEM((columns_here, HID), F32),
            pltpu.VMEM((2, 4, columns_here, HID // 2), F32),
            pltpu.VMEM((4, columns_here, HID // 2), F32),
            pltpu.VMEM((LEVELS, columns_here, HID), BF16),
            pltpu.VMEM((2, 4, 2 * columns_here, HID // 2), F32),
            pltpu.SemaphoreType.DMA(()),
        ),
    )
    return result.reshape(node_rows, node_cols, channels)


def solution(mesh):
    devices = mesh.devices
    mesh = jax.sharding.Mesh(devices.reshape(4, 4, 2, 4), ALL)
    placed = (
        P(ELEM, "x", None),
        P(ELEM, "x"),
        P(ALL, None),
        P(),
        P(),
        P(),
        P(),
        P(),
    )
    return jax.shard_map(
        shards, mesh=mesh, in_specs=placed, out_specs=P(ELEM, "x", None), check_vma=False
    )
```

```python
import math

import jax
import jax.numpy as jnp
import numpy as np
from jax import lax
from jax.experimental import pallas as pl
from jax.experimental.pallas import tpu as pltpu
from jax.sharding import PartitionSpec as P

NP = 4
NV = 4
HID = 512
LEVELS = 32
LANES = 128
COURANT = 0.05
F32 = jnp.float32
BF16 = jnp.bfloat16
UNR = 15
VMEM_LIMIT = 16 << 20


def gll_table():
    nodes = np.array([-1.0, -1.0 / math.sqrt(5.0), 1.0 / math.sqrt(5.0), 1.0])
    width = nodes.shape[0]
    table = np.zeros((width, width))
    for row in range(width):
        for column in range(width):
            if row != column:
                upper = np.prod(
                    [nodes[row] - nodes[other] for other in range(width) if other != row]
                )
                lower = np.prod(
                    [nodes[column] - nodes[other] for other in range(width) if other != column]
                )
                table[row, column] = upper / (lower * (nodes[row] - nodes[column]))
            else:
                table[row, row] = sum(
                    (1.0 / (nodes[row] - nodes[other]) for other in range(width) if other != row)
                )
    return table


D = [[float(v) for v in row] for row in gll_table()]


def winds(f):
    flat = f.reshape(-1, LANES)
    v = lax.broadcasted_iota(jnp.int32, flat.shape, 1) % NV
    one = pltpu.roll(flat, 1, 1)
    two = pltpu.roll(flat, 2, 1)
    three = pltpu.roll(flat, 3, 1)
    back = pltpu.roll(flat, LANES - 1, 1)
    first = jnp.where(v == 0, flat, jnp.where(v == 1, one, jnp.where(v == 2, two, three)))
    second = jnp.where(v == 0, back, jnp.where(v == 1, flat, jnp.where(v == 2, one, two)))
    return first.reshape(f.shape), second.reshape(f.shape)


def along_x(f):
    rows = f.reshape(f.shape[0] // NP, NP, f.shape[1], LANES)
    pieces = []
    for i in range(NP):
        total = D[i][0] * rows[:, 0]
        for k in range(1, NP):
            total = total + D[i][k] * rows[:, k]
        pieces.append(total)
    return jnp.stack(pieces, axis=1).reshape(f.shape)


def along_y(f):
    size = f.shape[1]
    y = lax.broadcasted_iota(jnp.int32, (1, size, LANES), 1) % NP
    total = None
    for shift in range(-(NP - 1), NP):
        factor = jnp.zeros((1, size, LANES), F32)
        for i in range(NP):
            if 0 <= i + shift < NP:
                factor = jnp.where(y == i, D[i][i + shift], factor)
        moved = f if shift == 0 else pltpu.roll(f, (-shift) % size, 1)
        term = factor * moved
        total = term if total is None else total + term
    return total


def average_y(f, left, right):
    size = f.shape[1]
    y = lax.broadcasted_iota(jnp.int32, (1, size, LANES), 1)
    ahead = pltpu.roll(f, size - 1, 1)
    behind = pltpu.roll(f, 1, 1)
    other = jnp.where(y % NP == NP - 1, ahead, jnp.where(y % NP == 0, behind, f))
    other = jnp.where(y == size - 1, right, jnp.where(y == 0, left, other))
    return (f + other) * 0.5


def average_x(f, before, after):
    rows = f.shape[0]
    pieces = []
    for r in range(rows):
        if r % NP == 0:
            other = before if r == 0 else f[r - 1]
            pieces.append((f[r] + other) * 0.5)
        elif r % NP == NP - 1:
            other = after if r == rows - 1 else f[r + 1]
            pieces.append((f[r] + other) * 0.5)
        else:
            pieces.append(f[r])
    return jnp.stack(pieces, axis=0)


def first_kernel(
    state_hbm, surface_hbm, moved_ref, to_core_ref, to_chip_ref, spread_ref, state_ref, surface_ref, arrived
):
    copies = (
        pltpu.make_async_copy(surface_hbm, surface_ref, arrived.at[0]),
        pltpu.make_async_copy(state_hbm, state_ref, arrived.at[1]),
    )
    for copy in copies:
        copy.start()
    copies[0].wait()
    spread_ref[...] = jnp.broadcast_to(surface_ref[...][None], spread_ref.shape)
    copies[1].wait()
    f = state_ref[...]
    wind_x, wind_y = winds(f)
    a = f - COURANT * (wind_x * along_x(f) + wind_y * along_y(f))
    moved_ref[...] = a
    n = a.shape[0]
    first = D[0][1] * a[1] + D[0][2] * a[2] + D[0][3] * ((a[3] + a[4]) * 0.5)
    last = D[3][0] * ((a[n - 4] + a[n - 5]) * 0.5) + D[3][1] * a[n - 3] + D[3][2] * a[n - 2]
    even = lax.axis_index("c") == 0
    to_core_ref[0] = jnp.where(even, a[n - 1], a[0])
    to_core_ref[1] = jnp.where(even, last, first)
    to_chip_ref[0] = jnp.where(even, a[0], a[n - 1])
    to_chip_ref[1] = jnp.where(even, first, last)


def sort_edges(core_ref, chip_ref):
    even = lax.axis_index("c") == 0
    core, chip = core_ref[...], chip_ref[...]
    return jnp.where(even, chip, core), jnp.where(even, core, chip)


def second_kernel(moved_ref, core_ref, chip_ref, g_ref, to_left_ref, to_right_ref):
    before, after = sort_edges(core_ref, chip_ref)
    g = average_x(moved_ref[...], before[0], after[0])
    g_ref[...] = g
    rows, size, _ = g.shape
    middle = (g[:, 3] + g[:, 4]) * 0.5
    to_left_ref[0:rows] = g[:, 0]
    to_left_ref[rows : 2 * rows] = D[0][1] * g[:, 1] + D[0][2] * g[:, 2] + D[0][3] * middle
    to_right_ref[0:rows] = g[:, size - 1]
    to_right_ref[rows : 2 * rows] = (
        D[3][0] * middle + D[3][1] * g[:, size - 3] + D[3][2] * g[:, size - 2]
    )
    up, down = before[1], after[1]
    y = lax.broadcasted_iota(jnp.int32, (size, LANES), 0)
    to_left_ref[2 * rows : 2 * rows + 8] = jnp.where(
        y == 0, up, jnp.where(y == 1, pltpu.roll(down, 1, 0), 0.0)
    )
    to_right_ref[2 * rows : 2 * rows + 8] = jnp.where(
        y == 0, pltpu.roll(up, 1, 0), jnp.where(y == 1, pltpu.roll(down, 2, 0), 0.0)
    )


def third_kernel(g_ref, core_ref, chip_ref, left_ref, right_ref, field_ref):
    before, after = sort_edges(core_ref, chip_ref)
    g = g_ref[...]
    rows, size, _ = g.shape
    left_g = left_ref[0:rows].reshape(rows, 1, LANES)
    right_g = right_ref[0:rows].reshape(rows, 1, LANES)
    f = average_y(g, left_g, right_g)
    tail_l = left_ref[2 * rows : 2 * rows + 8]
    tail_r = right_ref[2 * rows : 2 * rows + 8]
    up = average_y(before[1:2], tail_l[0:1].reshape(1, 1, LANES), tail_r[0:1].reshape(1, 1, LANES))[0]
    down = average_y(after[1:2], tail_l[1:2].reshape(1, 1, LANES), tail_r[1:2].reshape(1, 1, LANES))[0]
    slope_x = average_x(
        along_x(f), D[3][3] * f[0] + up, D[0][0] * f[rows - 1] + down
    )
    other_l = left_ref[rows : 2 * rows].reshape(rows, 1, LANES)
    other_r = right_ref[rows : 2 * rows].reshape(rows, 1, LANES)
    slope_y = average_y(along_y(f), D[3][3] * f + other_l, D[0][0] * f + other_r)
    wind_x, wind_y = winds(f)
    field_ref[...] = f - COURANT * (wind_x * slope_x + wind_y * slope_y)


def pick_owner(table_ref, pick, wanted, surf):
    peers, features, slot_count = table_ref.shape
    lane = lax.broadcasted_iota(jnp.int32, surf.shape, 1)
    for k in range(0, peers, 16):
        found = lax.dot_general(
            pick,
            table_ref[k : k + 16].reshape(16 * features, slot_count),
            (((1,), (1,)), ((), ())),
            preferred_element_type=F32,
        )
        for half in range(2):
            own = wanted == lane // features + (k + 8 * half)
            surf = jnp.where(own, found[:, half * LANES : (half + 1) * LANES], surf)
    return surf


def prepare_kernel(
    near_ref, slots_hbm, state_w_hbm, surf_w_hbm, hidden_w_hbm, bias_hbm,
    hidden_w_ref, in_w_ref, surf_ref, pick_ref, wanted_ref,
    slots_ref, state_w_ref, surf_w_ref, bias_ref, arrived,
):
    pairs = (
        (slots_hbm, slots_ref),
        (state_w_hbm, state_w_ref),
        (surf_w_hbm, surf_w_ref),
        (bias_hbm, bias_ref),
        (hidden_w_hbm, hidden_w_ref),
    )
    copies = [pltpu.make_async_copy(a, b, arrived.at[i]) for i, (a, b) in enumerate(pairs)]
    for copy in copies:
        copy.start()
    rows = surf_ref.shape[0]
    copies[0].wait()
    slots = slots_ref[...]
    slots = jnp.concatenate(
        [jnp.broadcast_to(slots[:, x : x + 1], (8, 2 * LANES)) for x in range(rows // 8)], axis=0
    )
    place = jnp.bitwise_and(slots, 255)
    owner = lax.shift_right_logical(slots[:, :LANES], 8)
    index = jnp.bitwise_or(
        lax.shift_left(lax.shift_right_logical(owner, 3), 2), jnp.bitwise_and(owner, 3)
    )
    here = jnp.bitwise_and(lax.shift_right_logical(owner, 2), 1) == lax.axis_index("c")
    pick = (lax.broadcasted_iota(jnp.int32, place.shape, 1) == place).astype(BF16)
    pick_ref[...] = pick
    wanted_ref[...] = jnp.where(here, -1, index)
    surf_ref[...] = pick_owner(
        near_ref, pick, jnp.where(here, index, -1), jnp.zeros((rows, LANES), F32)
    )
    for copy in copies[1:4]:
        copy.wait()
    row = lax.broadcasted_iota(jnp.int32, (64, NV), 0)
    col = lax.broadcasted_iota(jnp.int32, (64, NV), 1)
    spread = (row % NV == col).astype(BF16)
    in_w_ref[0:64] = jnp.dot(spread, state_w_ref[...], preferred_element_type=F32).astype(BF16)
    bias = bias_ref[...]
    high = bias.astype(BF16).astype(F32)
    rest = bias - high
    mid = rest.astype(BF16).astype(F32)
    low = rest - mid
    r = lax.broadcasted_iota(jnp.int32, (16, 1), 0)
    parts = jnp.where(r == 0, high, jnp.where(r == 1, mid, jnp.where(r == 2, low, 0.0)))
    in_w_ref[64:80] = parts.astype(BF16)
    in_w_ref[80:96] = surf_w_ref[...]
    in_w_ref[96:128] = jnp.zeros((32, 4 * HID), BF16)
    copies[4].wait()


def lstm_kernel(
    far_ref, field_ref, hidden_w_ref, in_w_ref, surf_ref, pick_ref, wanted_ref, out_w_hbm,
    out_ref, out_w_ref, cell_ref, part_ref, pend_ref, past_ref, feed_ref, arrived,
):
    copy = pltpu.make_async_copy(out_w_hbm, out_w_ref, arrived)
    copy.start()
    rows = field_ref.shape[0]
    features = far_ref.shape[1]
    unit = HID // 2
    surf = pick_owner(far_ref, pick_ref[...], wanted_ref[...], surf_ref[...])
    row = lax.broadcasted_iota(jnp.int32, (LANES, LANES), 0)
    col = lax.broadcasted_iota(jnp.int32, (LANES, LANES), 1)
    fold = (col - 80 == row % features).astype(BF16)
    surf = jnp.dot(surf.astype(BF16), fold, preferred_element_type=F32)
    lane = lax.broadcasted_iota(jnp.int32, (rows, LANES), 1)
    fixed = jnp.where((lane >= 64) & (lane < 67), 0.5, 0.5 * surf)
    field = field_ref[...]
    half_field = 0.5 * field.astype(BF16).astype(F32)
    swapped = pltpu.roll(half_field, 64, 1)

    def level_input(level):
        source = jnp.where(level < LEVELS // 2, half_field, swapped)
        return jnp.where(lane // NV == level % (LEVELS // 2), source, fixed).astype(BF16)

    def dot(a, b):
        return jnp.dot(a, b, preferred_element_type=F32)

    def cols(q, j):
        return slice(q * HID + j * unit, q * HID + (j + 1) * unit)

    def cell_step(g, j, first=False):
        s = slice(j * unit, (j + 1) * unit)
        c = (0.5 * jnp.tanh(g[0]) + 0.5) * jnp.tanh(g[2] + g[2])
        if not first:
            c = c + (0.5 * jnp.tanh(g[1]) + 0.5) * cell_ref[:, s]
        cell_ref[:, s] = c
        return ((0.25 * jnp.tanh(g[3]) + 0.25) * jnp.tanh(c)).astype(BF16)

    x = level_input(0)
    low_half = cell_step([dot(x, in_w_ref[:, cols(q, 0)]) for q in range(4)], 0, True)
    for q in range(4):
        pend_ref[q] = dot(x, in_w_ref[:, cols(q, 1)])
    cell_ref[:, unit:HID] = jnp.zeros((rows, unit), F32)

    def finish(level, low_half):
        high_half = cell_step([pend_ref[q] for q in range(4)], 1)
        past_ref[level] = jnp.concatenate([low_half, high_half], axis=1)
        return high_half

    def feed(level):
        x = jnp.concatenate([level_input(level), level_input(level + 1)], axis=0)
        for j in range(2):
            for q in range(4):
                feed_ref[j, q] = dot(x, in_w_ref[:, cols(q, j)])

    def two_steps(pair, low_half):
        level = 2 * pair + 1
        feed(level)
        return step(level + 1, 1, step(level, 0, low_half))

    def step(level, odd, low_half):
        for j in range(2):
            for q in range(4):
                part_ref[j, q] = feed_ref[j, q, odd * rows : (odd + 1) * rows] + dot(
                    low_half, hidden_w_ref[0:unit, cols(q, j)]
                )
        high_half = finish(level - 1, low_half)
        g = [
            part_ref[0, q] + dot(high_half, hidden_w_ref[unit:HID, cols(q, 0)]) for q in range(4)
        ]
        new = cell_step(g, 0)
        for q in range(4):
            pend_ref[q] = part_ref[1, q] + dot(high_half, hidden_w_ref[unit:HID, cols(q, 1)])
        return new

    low_half = lax.fori_loop(0, LEVELS // 2 - 1, two_steps, low_half, unroll=UNR)
    feed(LEVELS - 1)
    low_half = step(LEVELS - 1, 0, low_half)
    finish(LEVELS - 1, low_half)
    copy.wait()
    out_w = out_w_ref[...].astype(F32)
    out_w = jnp.concatenate([out_w + out_w, jnp.zeros((4, HID), F32)], axis=0).astype(BF16)
    gain = []
    for k in range(0, LEVELS, 8):
        p = lax.dot_general(
            out_w,
            past_ref[k : k + 8].reshape(8 * rows, HID),
            (((1,), (1,)), ((), ())),
            preferred_element_type=F32,
        )
        gain += [p[0:NV, i * rows : (i + 1) * rows] for i in range(8)]
    gain = jnp.concatenate(gain, axis=0).T
    out_ref[...] = field + gain.astype(BF16).astype(F32)


def call(kernel, out_shape, *args, kept=(), scratch=(), cost=None):
    placed = len(args)
    args = (*args, *[pltpu.with_memory_space_constraint(a, pltpu.HBM) for a in kept])
    return pl.pallas_call(
        kernel,
        out_shape=out_shape,
        in_specs=[
            pl.BlockSpec(memory_space=pltpu.VMEM if i < placed else pltpu.HBM)
            for i in range(len(args))
        ],
        out_specs=jax.tree.map(lambda _: pl.BlockSpec(memory_space=pltpu.VMEM), out_shape),
        scratch_shapes=list(scratch),
        compiler_params=pltpu.CompilerParams(vmem_limit_bytes=VMEM_LIMIT),
        cost_estimate=cost,
    )(*args)


def like(*shape, dtype=F32):
    return jax.ShapeDtypeStruct(shape, dtype)


ALL = ("z", "y", "c", "x")
ELEM = ("z", "y", "c")


def exchange(to_lower, to_upper, axes):
    size = math.prod(lax.axis_size(a) for a in axes)
    up = [(i, (i + 1) % size) for i in range(size)]
    down = [(j, i) for i, j in up]
    return lax.ppermute(to_upper, axes, up), lax.ppermute(to_lower, axes, down)


def shards(state, assignment, surface, w_state, w_surf, w_hidden, bias, w_out):
    node_rows, node_cols, channels = state.shape
    columns_here = node_rows * node_cols
    slot_count, features = surface.shape
    peers = lax.axis_size("z") * lax.axis_size("y") * lax.axis_size("x")
    block = like(node_rows, node_cols, channels)
    edge = like(2, node_cols, channels)
    moved, to_core, to_chip, spread = call(
        first_kernel,
        (block, edge, edge, like(peers, features, slot_count, dtype=BF16)),
        kept=(state, surface.T),
        scratch=(
            pltpu.VMEM(state.shape, F32),
            pltpu.VMEM((features, slot_count), BF16),
            pltpu.SemaphoreType.DMA((2,)),
        ),
    )
    core = lax.ppermute(to_core, "c", [(0, 1), (1, 0)])
    count = math.prod(lax.axis_size(a) for a in ELEM)
    pairs = [(i, (i + 1) % count) for i in range(1, count, 2)]
    chip = lax.ppermute(to_chip, ELEM, pairs + [(j, i) for i, j in pairs])
    near = lax.all_to_all(spread, ("z", "y", "x"), split_axis=0, concat_axis=0, tiled=True)
    side = like(2 * node_rows + 8, channels)
    g, to_left, to_right = call(
        second_kernel,
        (block, side, side),
        moved,
        core,
        chip,
    )
    left, right = exchange(to_left, to_right, ("x",))
    field = call(third_kernel, block, g, core, chip, left, right)
    near, _ = lax.optimization_barrier((near, field))
    far = lax.ppermute(near, "c", [(0, 1), (1, 0)])
    kept = (assignment.T, w_state, w_surf, w_hidden, bias.reshape(1, 4 * HID))
    prepared = call(
        prepare_kernel,
        (
            like(HID, 4 * HID, dtype=BF16),
            like(LANES, 4 * HID, dtype=BF16),
            like(columns_here, LANES),
            like(columns_here, slot_count, dtype=BF16),
            like(columns_here, LANES, dtype=jnp.int32),
        ),
        near,
        kept=kept,
        scratch=(
            *[pltpu.VMEM(a.shape, a.dtype) for i, a in enumerate(kept) if i != 3],
            pltpu.SemaphoreType.DMA((len(kept),)),
        ),
        cost=pl.CostEstimate(flops=1 << 28, bytes_accessed=4 << 20, transcendentals=0),
    )
    result = call(
        lstm_kernel,
        like(columns_here, channels),
        far,
        field.reshape(columns_here, channels),
        *prepared,
        kept=(w_out.T,),
        scratch=(
            pltpu.VMEM((NV, HID), BF16),
            pltpu.VMEM((columns_here, HID), F32),
            pltpu.VMEM((2, 4, columns_here, HID // 2), F32),
            pltpu.VMEM((4, columns_here, HID // 2), F32),
            pltpu.VMEM((LEVELS, columns_here, HID), BF16),
            pltpu.VMEM((2, 4, 2 * columns_here, HID // 2), F32),
            pltpu.SemaphoreType.DMA(()),
        ),
    )
    return result.reshape(node_rows, node_cols, channels)


def solution(mesh):
    devices = mesh.devices
    mesh = jax.sharding.Mesh(devices.reshape(4, 4, 2, 4), ALL)
    placed = (
        P(ELEM, "x", None),
        P(ELEM, "x"),
        P(ALL, None),
        P(),
        P(),
        P(),
        P(),
        P(),
    )
    return jax.shard_map(
        shards, mesh=mesh, in_specs=placed, out_specs=P(ELEM, "x", None), check_vma=False
    )
```

```python
import math

import jax
import jax.numpy as jnp
import numpy as np
from jax import lax
from jax.experimental import pallas as pl
from jax.experimental.pallas import tpu as pltpu
from jax.sharding import PartitionSpec as P

NP = 4
NV = 4
HID = 512
LEVELS = 32
LANES = 128
COURANT = 0.05
F32 = jnp.float32
BF16 = jnp.bfloat16
VMEM_LIMIT = 16 << 20


def gll_table():
    nodes = np.array([-1.0, -1.0 / math.sqrt(5.0), 1.0 / math.sqrt(5.0), 1.0])
    width = nodes.shape[0]
    table = np.zeros((width, width))
    for row in range(width):
        for column in range(width):
            if row != column:
                upper = np.prod(
                    [nodes[row] - nodes[other] for other in range(width) if other != row]
                )
                lower = np.prod(
                    [nodes[column] - nodes[other] for other in range(width) if other != column]
                )
                table[row, column] = upper / (lower * (nodes[row] - nodes[column]))
            else:
                table[row, row] = sum(
                    (1.0 / (nodes[row] - nodes[other]) for other in range(width) if other != row)
                )
    return table


D = [[float(v) for v in row] for row in gll_table()]


def winds(f):
    flat = f.reshape(-1, LANES)
    v = lax.broadcasted_iota(jnp.int32, flat.shape, 1) % NV
    one = pltpu.roll(flat, 1, 1)
    two = pltpu.roll(flat, 2, 1)
    three = pltpu.roll(flat, 3, 1)
    back = pltpu.roll(flat, LANES - 1, 1)
    first = jnp.where(v == 0, flat, jnp.where(v == 1, one, jnp.where(v == 2, two, three)))
    second = jnp.where(v == 0, back, jnp.where(v == 1, flat, jnp.where(v == 2, one, two)))
    return first.reshape(f.shape), second.reshape(f.shape)


def along_x(f):
    rows = f.reshape(f.shape[0] // NP, NP, f.shape[1], LANES)
    pieces = []
    for i in range(NP):
        total = D[i][0] * rows[:, 0]
        for k in range(1, NP):
            total = total + D[i][k] * rows[:, k]
        pieces.append(total)
    return jnp.stack(pieces, axis=1).reshape(f.shape)


def along_y(f):
    size = f.shape[1]
    y = lax.broadcasted_iota(jnp.int32, (1, size, LANES), 1) % NP
    total = None
    for shift in range(-(NP - 1), NP):
        factor = jnp.zeros((1, size, LANES), F32)
        for i in range(NP):
            if 0 <= i + shift < NP:
                factor = jnp.where(y == i, D[i][i + shift], factor)
        moved = f if shift == 0 else pltpu.roll(f, (-shift) % size, 1)
        term = factor * moved
        total = term if total is None else total + term
    return total


def average_y(f, left, right):
    size = f.shape[1]
    y = lax.broadcasted_iota(jnp.int32, (1, size, LANES), 1)
    ahead = pltpu.roll(f, size - 1, 1)
    behind = pltpu.roll(f, 1, 1)
    other = jnp.where(y % NP == NP - 1, ahead, jnp.where(y % NP == 0, behind, f))
    other = jnp.where(y == size - 1, right, jnp.where(y == 0, left, other))
    return (f + other) * 0.5


def average_x(f, before, after):
    rows = f.shape[0]
    pieces = []
    for r in range(rows):
        if r % NP == 0:
            other = before if r == 0 else f[r - 1]
            pieces.append((f[r] + other) * 0.5)
        elif r % NP == NP - 1:
            other = after if r == rows - 1 else f[r + 1]
            pieces.append((f[r] + other) * 0.5)
        else:
            pieces.append(f[r])
    return jnp.stack(pieces, axis=0)


def first_kernel(
    state_hbm, surface_hbm, moved_ref, to_core_ref, to_chip_ref, spread_ref, state_ref, surface_ref, arrived
):
    copies = (
        pltpu.make_async_copy(surface_hbm, surface_ref, arrived.at[0]),
        pltpu.make_async_copy(state_hbm, state_ref, arrived.at[1]),
    )
    for copy in copies:
        copy.start()
    copies[0].wait()
    spread_ref[...] = jnp.broadcast_to(surface_ref[...][None], spread_ref.shape)
    copies[1].wait()
    f = state_ref[...]
    wind_x, wind_y = winds(f)
    a = f - COURANT * (wind_x * along_x(f) + wind_y * along_y(f))
    moved_ref[...] = a
    n = a.shape[0]
    first = D[0][1] * a[1] + D[0][2] * a[2] + D[0][3] * ((a[3] + a[4]) * 0.5)
    last = D[3][0] * ((a[n - 4] + a[n - 5]) * 0.5) + D[3][1] * a[n - 3] + D[3][2] * a[n - 2]
    even = lax.axis_index("c") == 0
    to_core_ref[0] = jnp.where(even, a[n - 1], a[0])
    to_core_ref[1] = jnp.where(even, last, first)
    to_chip_ref[0] = jnp.where(even, a[0], a[n - 1])
    to_chip_ref[1] = jnp.where(even, first, last)


def sort_edges(core_ref, chip_ref):
    even = lax.axis_index("c") == 0
    core, chip = core_ref[...], chip_ref[...]
    return jnp.where(even, chip, core), jnp.where(even, core, chip)


def second_kernel(moved_ref, core_ref, chip_ref, g_ref, to_left_ref, to_right_ref):
    before, after = sort_edges(core_ref, chip_ref)
    g = average_x(moved_ref[...], before[0], after[0])
    g_ref[...] = g
    rows, size, _ = g.shape
    middle = (g[:, 3] + g[:, 4]) * 0.5
    to_left_ref[0:rows] = g[:, 0]
    to_left_ref[rows : 2 * rows] = D[0][1] * g[:, 1] + D[0][2] * g[:, 2] + D[0][3] * middle
    to_right_ref[0:rows] = g[:, size - 1]
    to_right_ref[rows : 2 * rows] = (
        D[3][0] * middle + D[3][1] * g[:, size - 3] + D[3][2] * g[:, size - 2]
    )
    up, down = before[1], after[1]
    y = lax.broadcasted_iota(jnp.int32, (size, LANES), 0)
    to_left_ref[2 * rows : 2 * rows + 8] = jnp.where(
        y == 0, up, jnp.where(y == 1, pltpu.roll(down, 1, 0), 0.0)
    )
    to_right_ref[2 * rows : 2 * rows + 8] = jnp.where(
        y == 0, pltpu.roll(up, 1, 0), jnp.where(y == 1, pltpu.roll(down, 2, 0), 0.0)
    )


def third_kernel(g_ref, core_ref, chip_ref, left_ref, right_ref, field_ref):
    before, after = sort_edges(core_ref, chip_ref)
    g = g_ref[...]
    rows, size, _ = g.shape
    left_g = left_ref[0:rows].reshape(rows, 1, LANES)
    right_g = right_ref[0:rows].reshape(rows, 1, LANES)
    f = average_y(g, left_g, right_g)
    tail_l = left_ref[2 * rows : 2 * rows + 8]
    tail_r = right_ref[2 * rows : 2 * rows + 8]
    up = average_y(before[1:2], tail_l[0:1].reshape(1, 1, LANES), tail_r[0:1].reshape(1, 1, LANES))[0]
    down = average_y(after[1:2], tail_l[1:2].reshape(1, 1, LANES), tail_r[1:2].reshape(1, 1, LANES))[0]
    slope_x = average_x(
        along_x(f), D[3][3] * f[0] + up, D[0][0] * f[rows - 1] + down
    )
    other_l = left_ref[rows : 2 * rows].reshape(rows, 1, LANES)
    other_r = right_ref[rows : 2 * rows].reshape(rows, 1, LANES)
    slope_y = average_y(along_y(f), D[3][3] * f + other_l, D[0][0] * f + other_r)
    wind_x, wind_y = winds(f)
    field_ref[...] = f - COURANT * (wind_x * slope_x + wind_y * slope_y)


def pick_owner(table_ref, pick, wanted, surf):
    peers, features, slot_count = table_ref.shape
    lane = lax.broadcasted_iota(jnp.int32, surf.shape, 1)
    for k in range(0, peers, 16):
        found = lax.dot_general(
            pick,
            table_ref[k : k + 16].reshape(16 * features, slot_count),
            (((1,), (1,)), ((), ())),
            preferred_element_type=F32,
        )
        for half in range(2):
            own = wanted == lane // features + (k + 8 * half)
            surf = jnp.where(own, found[:, half * LANES : (half + 1) * LANES], surf)
    return surf


def prepare_kernel(
    near_ref, slots_hbm, state_w_hbm, surf_w_hbm, hidden_w_hbm, bias_hbm,
    hidden_w_ref, in_w_ref, surf_ref, pick_ref, wanted_ref,
    slots_ref, state_w_ref, surf_w_ref, bias_ref, arrived,
):
    pairs = (
        (slots_hbm, slots_ref),
        (state_w_hbm, state_w_ref),
        (surf_w_hbm, surf_w_ref),
        (bias_hbm, bias_ref),
        (hidden_w_hbm, hidden_w_ref),
    )
    copies = [pltpu.make_async_copy(a, b, arrived.at[i]) for i, (a, b) in enumerate(pairs)]
    for copy in copies:
        copy.start()
    rows = surf_ref.shape[0]
    copies[0].wait()
    slots = slots_ref[...]
    slots = jnp.concatenate(
        [jnp.broadcast_to(slots[:, x : x + 1], (8, 2 * LANES)) for x in range(rows // 8)], axis=0
    )
    place = jnp.bitwise_and(slots, 255)
    owner = lax.shift_right_logical(slots[:, :LANES], 8)
    index = jnp.bitwise_or(
        lax.shift_left(lax.shift_right_logical(owner, 3), 2), jnp.bitwise_and(owner, 3)
    )
    here = jnp.bitwise_and(lax.shift_right_logical(owner, 2), 1) == lax.axis_index("c")
    pick = (lax.broadcasted_iota(jnp.int32, place.shape, 1) == place).astype(BF16)
    pick_ref[...] = pick
    wanted_ref[...] = jnp.where(here, -1, index)
    surf_ref[...] = pick_owner(
        near_ref, pick, jnp.where(here, index, -1), jnp.zeros((rows, LANES), F32)
    )
    for copy in copies[1:4]:
        copy.wait()
    row = lax.broadcasted_iota(jnp.int32, (64, NV), 0)
    col = lax.broadcasted_iota(jnp.int32, (64, NV), 1)
    spread = (row % NV == col).astype(BF16)
    in_w_ref[0:64] = jnp.dot(spread, state_w_ref[...], preferred_element_type=F32).astype(BF16)
    bias = bias_ref[...]
    high = bias.astype(BF16).astype(F32)
    rest = bias - high
    mid = rest.astype(BF16).astype(F32)
    low = rest - mid
    r = lax.broadcasted_iota(jnp.int32, (16, 1), 0)
    parts = jnp.where(r == 0, high, jnp.where(r == 1, mid, jnp.where(r == 2, low, 0.0)))
    in_w_ref[64:80] = parts.astype(BF16)
    in_w_ref[80:96] = surf_w_ref[...]
    in_w_ref[96:128] = jnp.zeros((32, 4 * HID), BF16)
    copies[4].wait()


def lstm_kernel(
    far_ref, field_ref, hidden_w_ref, in_w_ref, surf_ref, pick_ref, wanted_ref, out_w_hbm,
    out_ref, out_w_ref, cell_ref, part_ref, pend_ref, past_ref, feed_ref, arrived,
):
    copy = pltpu.make_async_copy(out_w_hbm, out_w_ref, arrived)
    copy.start()
    rows = field_ref.shape[0]
    features = far_ref.shape[1]
    unit = HID // 2
    surf = pick_owner(far_ref, pick_ref[...], wanted_ref[...], surf_ref[...])
    row = lax.broadcasted_iota(jnp.int32, (LANES, LANES), 0)
    col = lax.broadcasted_iota(jnp.int32, (LANES, LANES), 1)
    fold = (col - 80 == row % features).astype(BF16)
    surf = jnp.dot(surf.astype(BF16), fold, preferred_element_type=F32)
    lane = lax.broadcasted_iota(jnp.int32, (rows, LANES), 1)
    fixed = jnp.where((lane >= 64) & (lane < 67), 0.5, 0.5 * surf)
    field = field_ref[...]
    half_field = 0.5 * field.astype(BF16).astype(F32)
    swapped = pltpu.roll(half_field, 64, 1)

    def level_input(level):
        source = jnp.where(level < LEVELS // 2, half_field, swapped)
        return jnp.where(lane // NV == level % (LEVELS // 2), source, fixed).astype(BF16)

    def dot(a, b):
        return jnp.dot(a, b, preferred_element_type=F32)

    def cols(q, j):
        return slice(q * HID + j * unit, q * HID + (j + 1) * unit)

    def cell_step(g, j, first=False):
        s = slice(j * unit, (j + 1) * unit)
        c = (0.5 * jnp.tanh(g[0]) + 0.5) * jnp.tanh(g[2] + g[2])
        if not first:
            c = c + (0.5 * jnp.tanh(g[1]) + 0.5) * cell_ref[:, s]
        cell_ref[:, s] = c
        return ((0.25 * jnp.tanh(g[3]) + 0.25) * jnp.tanh(c)).astype(BF16)

    x = level_input(0)
    low_half = cell_step([dot(x, in_w_ref[:, cols(q, 0)]) for q in range(4)], 0, True)
    for q in range(4):
        pend_ref[q] = dot(x, in_w_ref[:, cols(q, 1)])
    cell_ref[:, unit:HID] = jnp.zeros((rows, unit), F32)

    def finish(level, low_half):
        high_half = cell_step([pend_ref[q] for q in range(4)], 1)
        past_ref[level] = jnp.concatenate([low_half, high_half], axis=1)
        return high_half

    def step(level, low_half):
        x = level_input(level)
        for j in range(2):
            for q in range(4):
                feed_ref[j, q] = dot(x, in_w_ref[:, cols(q, j)])
        for j in range(2):
            for q in range(4):
                part_ref[j, q] = feed_ref[j, q] + dot(low_half, hidden_w_ref[0:unit, cols(q, j)])
        high_half = finish(level - 1, low_half)
        g = [
            part_ref[0, q] + dot(high_half, hidden_w_ref[unit:HID, cols(q, 0)]) for q in range(4)
        ]
        new = cell_step(g, 0)
        for q in range(4):
            pend_ref[q] = part_ref[1, q] + dot(high_half, hidden_w_ref[unit:HID, cols(q, 1)])
        return new

    low_half = lax.fori_loop(1, LEVELS, step, low_half, unroll=LEVELS - 1)
    finish(LEVELS - 1, low_half)
    copy.wait()
    out_w = out_w_ref[...].astype(F32)
    out_w = jnp.concatenate([out_w + out_w, jnp.zeros((4, HID), F32)], axis=0).astype(BF16)
    gain = []
    for k in range(0, LEVELS, 8):
        p = lax.dot_general(
            out_w,
            past_ref[k : k + 8].reshape(8 * rows, HID),
            (((1,), (1,)), ((), ())),
            preferred_element_type=F32,
        )
        gain += [p[0:NV, i * rows : (i + 1) * rows] for i in range(8)]
    gain = jnp.concatenate(gain, axis=0).T
    out_ref[...] = field + gain.astype(BF16).astype(F32)


def call(kernel, out_shape, *args, kept=(), scratch=(), cost=None):
    placed = len(args)
    args = (*args, *[pltpu.with_memory_space_constraint(a, pltpu.HBM) for a in kept])
    return pl.pallas_call(
        kernel,
        out_shape=out_shape,
        in_specs=[
            pl.BlockSpec(memory_space=pltpu.VMEM if i < placed else pltpu.HBM)
            for i in range(len(args))
        ],
        out_specs=jax.tree.map(lambda _: pl.BlockSpec(memory_space=pltpu.VMEM), out_shape),
        scratch_shapes=list(scratch),
        compiler_params=pltpu.CompilerParams(vmem_limit_bytes=VMEM_LIMIT),
        cost_estimate=cost,
    )(*args)


def like(*shape, dtype=F32):
    return jax.ShapeDtypeStruct(shape, dtype)


ALL = ("z", "y", "c", "x")
ELEM = ("z", "y", "c")


def exchange(to_lower, to_upper, axes):
    size = math.prod(lax.axis_size(a) for a in axes)
    up = [(i, (i + 1) % size) for i in range(size)]
    down = [(j, i) for i, j in up]
    return lax.ppermute(to_upper, axes, up), lax.ppermute(to_lower, axes, down)


def shards(state, assignment, surface, w_state, w_surf, w_hidden, bias, w_out):
    node_rows, node_cols, channels = state.shape
    columns_here = node_rows * node_cols
    slot_count, features = surface.shape
    peers = lax.axis_size("z") * lax.axis_size("y") * lax.axis_size("x")
    block = like(node_rows, node_cols, channels)
    edge = like(2, node_cols, channels)
    moved, to_core, to_chip, spread = call(
        first_kernel,
        (block, edge, edge, like(peers, features, slot_count, dtype=BF16)),
        kept=(state, surface.T),
        scratch=(
            pltpu.VMEM(state.shape, F32),
            pltpu.VMEM((features, slot_count), BF16),
            pltpu.SemaphoreType.DMA((2,)),
        ),
    )
    core = lax.ppermute(to_core, "c", [(0, 1), (1, 0)])
    count = math.prod(lax.axis_size(a) for a in ELEM)
    pairs = [(i, (i + 1) % count) for i in range(1, count, 2)]
    chip = lax.ppermute(to_chip, ELEM, pairs + [(j, i) for i, j in pairs])
    near = lax.all_to_all(spread, ("z", "y", "x"), split_axis=0, concat_axis=0, tiled=True)
    side = like(2 * node_rows + 8, channels)
    g, to_left, to_right = call(
        second_kernel,
        (block, side, side),
        moved,
        core,
        chip,
    )
    left, right = exchange(to_left, to_right, ("x",))
    field = call(third_kernel, block, g, core, chip, left, right)
    near, _ = lax.optimization_barrier((near, field))
    far = lax.ppermute(near, "c", [(0, 1), (1, 0)])
    kept = (assignment.T, w_state, w_surf, w_hidden, bias.reshape(1, 4 * HID))
    prepared = call(
        prepare_kernel,
        (
            like(HID, 4 * HID, dtype=BF16),
            like(LANES, 4 * HID, dtype=BF16),
            like(columns_here, LANES),
            like(columns_here, slot_count, dtype=BF16),
            like(columns_here, LANES, dtype=jnp.int32),
        ),
        near,
        kept=kept,
        scratch=(
            *[pltpu.VMEM(a.shape, a.dtype) for i, a in enumerate(kept) if i != 3],
            pltpu.SemaphoreType.DMA((len(kept),)),
        ),
        cost=pl.CostEstimate(flops=1 << 28, bytes_accessed=4 << 20, transcendentals=0),
    )
    result = call(
        lstm_kernel,
        like(columns_here, channels),
        far,
        field.reshape(columns_here, channels),
        *prepared,
        kept=(w_out.T,),
        scratch=(
            pltpu.VMEM((NV, HID), BF16),
            pltpu.VMEM((columns_here, HID), F32),
            pltpu.VMEM((2, 4, columns_here, HID // 2), F32),
            pltpu.VMEM((4, columns_here, HID // 2), F32),
            pltpu.VMEM((LEVELS, columns_here, HID), BF16),
            pltpu.VMEM((2, 4, columns_here, HID // 2), F32),
            pltpu.SemaphoreType.DMA(()),
        ),
    )
    return result.reshape(node_rows, node_cols, channels)


def solution(mesh):
    devices = mesh.devices
    mesh = jax.sharding.Mesh(devices.reshape(4, 4, 2, 4), ALL)
    placed = (
        P(ELEM, "x", None),
        P(ELEM, "x"),
        P(ALL, None),
        P(),
        P(),
        P(),
        P(),
        P(),
    )
    return jax.shard_map(
        shards, mesh=mesh, in_specs=placed, out_specs=P(ELEM, "x", None), check_vma=False
    )
```

```python
import math

import jax
import jax.numpy as jnp
import numpy as np
from jax import lax
from jax.experimental import pallas as pl
from jax.experimental.pallas import tpu as pltpu
from jax.sharding import PartitionSpec as P

NP = 4
NV = 4
HID = 512
LEVELS = 32
LANES = 128
COURANT = 0.05
F32 = jnp.float32
BF16 = jnp.bfloat16
GROUP = 8
VMEM_LIMIT = 16 << 20


def gll_table():
    nodes = np.array([-1.0, -1.0 / math.sqrt(5.0), 1.0 / math.sqrt(5.0), 1.0])
    width = nodes.shape[0]
    table = np.zeros((width, width))
    for row in range(width):
        for column in range(width):
            if row != column:
                upper = np.prod(
                    [nodes[row] - nodes[other] for other in range(width) if other != row]
                )
                lower = np.prod(
                    [nodes[column] - nodes[other] for other in range(width) if other != column]
                )
                table[row, column] = upper / (lower * (nodes[row] - nodes[column]))
            else:
                table[row, row] = sum(
                    (1.0 / (nodes[row] - nodes[other]) for other in range(width) if other != row)
                )
    return table


D = [[float(v) for v in row] for row in gll_table()]


def winds(f):
    flat = f.reshape(-1, LANES)
    v = lax.broadcasted_iota(jnp.int32, flat.shape, 1) % NV
    one = pltpu.roll(flat, 1, 1)
    two = pltpu.roll(flat, 2, 1)
    three = pltpu.roll(flat, 3, 1)
    back = pltpu.roll(flat, LANES - 1, 1)
    first = jnp.where(v == 0, flat, jnp.where(v == 1, one, jnp.where(v == 2, two, three)))
    second = jnp.where(v == 0, back, jnp.where(v == 1, flat, jnp.where(v == 2, one, two)))
    return first.reshape(f.shape), second.reshape(f.shape)


def along_x(f):
    rows = f.reshape(f.shape[0] // NP, NP, f.shape[1], LANES)
    pieces = []
    for i in range(NP):
        total = D[i][0] * rows[:, 0]
        for k in range(1, NP):
            total = total + D[i][k] * rows[:, k]
        pieces.append(total)
    return jnp.stack(pieces, axis=1).reshape(f.shape)


def along_y(f):
    size = f.shape[1]
    y = lax.broadcasted_iota(jnp.int32, (1, size, LANES), 1) % NP
    total = None
    for shift in range(-(NP - 1), NP):
        factor = jnp.zeros((1, size, LANES), F32)
        for i in range(NP):
            if 0 <= i + shift < NP:
                factor = jnp.where(y == i, D[i][i + shift], factor)
        moved = f if shift == 0 else pltpu.roll(f, (-shift) % size, 1)
        term = factor * moved
        total = term if total is None else total + term
    return total


def average_y(f, left, right):
    size = f.shape[1]
    y = lax.broadcasted_iota(jnp.int32, (1, size, LANES), 1)
    ahead = pltpu.roll(f, size - 1, 1)
    behind = pltpu.roll(f, 1, 1)
    other = jnp.where(y % NP == NP - 1, ahead, jnp.where(y % NP == 0, behind, f))
    other = jnp.where(y == size - 1, right, jnp.where(y == 0, left, other))
    return (f + other) * 0.5


def average_x(f, before, after):
    rows = f.shape[0]
    pieces = []
    for r in range(rows):
        if r % NP == 0:
            other = before if r == 0 else f[r - 1]
            pieces.append((f[r] + other) * 0.5)
        elif r % NP == NP - 1:
            other = after if r == rows - 1 else f[r + 1]
            pieces.append((f[r] + other) * 0.5)
        else:
            pieces.append(f[r])
    return jnp.stack(pieces, axis=0)


def first_kernel(
    state_hbm, surface_hbm, moved_ref, to_core_ref, to_chip_ref, spread_ref, state_ref, surface_ref, arrived
):
    copies = (
        pltpu.make_async_copy(surface_hbm, surface_ref, arrived.at[0]),
        pltpu.make_async_copy(state_hbm, state_ref, arrived.at[1]),
    )
    for copy in copies:
        copy.start()
    copies[0].wait()
    spread_ref[...] = jnp.broadcast_to(surface_ref[...][None], spread_ref.shape)
    copies[1].wait()
    f = state_ref[...]
    wind_x, wind_y = winds(f)
    a = f - COURANT * (wind_x * along_x(f) + wind_y * along_y(f))
    moved_ref[...] = a
    n = a.shape[0]
    first = D[0][1] * a[1] + D[0][2] * a[2] + D[0][3] * ((a[3] + a[4]) * 0.5)
    last = D[3][0] * ((a[n - 4] + a[n - 5]) * 0.5) + D[3][1] * a[n - 3] + D[3][2] * a[n - 2]
    even = lax.axis_index("c") == 0
    to_core_ref[0] = jnp.where(even, a[n - 1], a[0])
    to_core_ref[1] = jnp.where(even, last, first)
    to_chip_ref[0] = jnp.where(even, a[0], a[n - 1])
    to_chip_ref[1] = jnp.where(even, first, last)


def sort_edges(core_ref, chip_ref):
    even = lax.axis_index("c") == 0
    core, chip = core_ref[...], chip_ref[...]
    return jnp.where(even, chip, core), jnp.where(even, core, chip)


def second_kernel(moved_ref, core_ref, chip_ref, g_ref, to_left_ref, to_right_ref):
    before, after = sort_edges(core_ref, chip_ref)
    g = average_x(moved_ref[...], before[0], after[0])
    g_ref[...] = g
    rows, size, _ = g.shape
    middle = (g[:, 3] + g[:, 4]) * 0.5
    to_left_ref[0:rows] = g[:, 0]
    to_left_ref[rows : 2 * rows] = D[0][1] * g[:, 1] + D[0][2] * g[:, 2] + D[0][3] * middle
    to_right_ref[0:rows] = g[:, size - 1]
    to_right_ref[rows : 2 * rows] = (
        D[3][0] * middle + D[3][1] * g[:, size - 3] + D[3][2] * g[:, size - 2]
    )
    up, down = before[1], after[1]
    y = lax.broadcasted_iota(jnp.int32, (size, LANES), 0)
    to_left_ref[2 * rows : 2 * rows + 8] = jnp.where(
        y == 0, up, jnp.where(y == 1, pltpu.roll(down, 1, 0), 0.0)
    )
    to_right_ref[2 * rows : 2 * rows + 8] = jnp.where(
        y == 0, pltpu.roll(up, 1, 0), jnp.where(y == 1, pltpu.roll(down, 2, 0), 0.0)
    )


def third_kernel(g_ref, core_ref, chip_ref, left_ref, right_ref, field_ref):
    before, after = sort_edges(core_ref, chip_ref)
    g = g_ref[...]
    rows, size, _ = g.shape
    left_g = left_ref[0:rows].reshape(rows, 1, LANES)
    right_g = right_ref[0:rows].reshape(rows, 1, LANES)
    f = average_y(g, left_g, right_g)
    tail_l = left_ref[2 * rows : 2 * rows + 8]
    tail_r = right_ref[2 * rows : 2 * rows + 8]
    up = average_y(before[1:2], tail_l[0:1].reshape(1, 1, LANES), tail_r[0:1].reshape(1, 1, LANES))[0]
    down = average_y(after[1:2], tail_l[1:2].reshape(1, 1, LANES), tail_r[1:2].reshape(1, 1, LANES))[0]
    slope_x = average_x(
        along_x(f), D[3][3] * f[0] + up, D[0][0] * f[rows - 1] + down
    )
    other_l = left_ref[rows : 2 * rows].reshape(rows, 1, LANES)
    other_r = right_ref[rows : 2 * rows].reshape(rows, 1, LANES)
    slope_y = average_y(along_y(f), D[3][3] * f + other_l, D[0][0] * f + other_r)
    wind_x, wind_y = winds(f)
    field_ref[...] = f - COURANT * (wind_x * slope_x + wind_y * slope_y)


def pick_owner(table_ref, pick, wanted, surf):
    peers, features, slot_count = table_ref.shape
    lane = lax.broadcasted_iota(jnp.int32, surf.shape, 1)
    for k in range(0, peers, 16):
        found = lax.dot_general(
            pick,
            table_ref[k : k + 16].reshape(16 * features, slot_count),
            (((1,), (1,)), ((), ())),
            preferred_element_type=F32,
        )
        for half in range(2):
            own = wanted == lane // features + (k + 8 * half)
            surf = jnp.where(own, found[:, half * LANES : (half + 1) * LANES], surf)
    return surf


def prepare_kernel(
    near_ref, slots_hbm, state_w_hbm, surf_w_hbm, hidden_w_hbm, bias_hbm,
    hidden_w_ref, in_w_ref, surf_ref, pick_ref, wanted_ref,
    slots_ref, state_w_ref, surf_w_ref, bias_ref, arrived,
):
    pairs = (
        (slots_hbm, slots_ref),
        (state_w_hbm, state_w_ref),
        (surf_w_hbm, surf_w_ref),
        (bias_hbm, bias_ref),
        (hidden_w_hbm, hidden_w_ref),
    )
    copies = [pltpu.make_async_copy(a, b, arrived.at[i]) for i, (a, b) in enumerate(pairs)]
    for copy in copies:
        copy.start()
    rows = surf_ref.shape[0]
    copies[0].wait()
    slots = slots_ref[...]
    slots = jnp.concatenate(
        [jnp.broadcast_to(slots[:, x : x + 1], (8, 2 * LANES)) for x in range(rows // 8)], axis=0
    )
    place = jnp.bitwise_and(slots, 255)
    owner = lax.shift_right_logical(slots[:, :LANES], 8)
    index = jnp.bitwise_or(
        lax.shift_left(lax.shift_right_logical(owner, 3), 2), jnp.bitwise_and(owner, 3)
    )
    here = jnp.bitwise_and(lax.shift_right_logical(owner, 2), 1) == lax.axis_index("c")
    pick = (lax.broadcasted_iota(jnp.int32, place.shape, 1) == place).astype(BF16)
    pick_ref[...] = pick
    wanted_ref[...] = jnp.where(here, -1, index)
    surf_ref[...] = pick_owner(
        near_ref, pick, jnp.where(here, index, -1), jnp.zeros((rows, LANES), F32)
    )
    for copy in copies[1:4]:
        copy.wait()
    row = lax.broadcasted_iota(jnp.int32, (64, NV), 0)
    col = lax.broadcasted_iota(jnp.int32, (64, NV), 1)
    spread = (row % NV == col).astype(BF16)
    in_w_ref[0:64] = jnp.dot(spread, state_w_ref[...], preferred_element_type=F32).astype(BF16)
    bias = bias_ref[...]
    high = bias.astype(BF16).astype(F32)
    rest = bias - high
    mid = rest.astype(BF16).astype(F32)
    low = rest - mid
    r = lax.broadcasted_iota(jnp.int32, (16, 1), 0)
    parts = jnp.where(r == 0, high, jnp.where(r == 1, mid, jnp.where(r == 2, low, 0.0)))
    in_w_ref[64:80] = parts.astype(BF16)
    in_w_ref[80:96] = surf_w_ref[...]
    in_w_ref[96:128] = jnp.zeros((32, 4 * HID), BF16)
    copies[4].wait()


def lstm_kernel(
    far_ref, field_ref, hidden_w_ref, in_w_ref, surf_ref, pick_ref, wanted_ref, out_w_hbm,
    out_ref, out_w_ref, cell_ref, part_ref, pend_ref, past_ref, feed_ref, arrived,
):
    copy = pltpu.make_async_copy(out_w_hbm, out_w_ref, arrived)
    copy.start()
    rows = field_ref.shape[0]
    features = far_ref.shape[1]
    unit = HID // 2
    surf = pick_owner(far_ref, pick_ref[...], wanted_ref[...], surf_ref[...])
    row = lax.broadcasted_iota(jnp.int32, (LANES, LANES), 0)
    col = lax.broadcasted_iota(jnp.int32, (LANES, LANES), 1)
    fold = (col - 80 == row % features).astype(BF16)
    surf = jnp.dot(surf.astype(BF16), fold, preferred_element_type=F32)
    lane = lax.broadcasted_iota(jnp.int32, (rows, LANES), 1)
    fixed = jnp.where((lane >= 64) & (lane < 67), 0.5, 0.5 * surf)
    field = field_ref[...]
    half_field = 0.5 * field.astype(BF16).astype(F32)
    swapped = pltpu.roll(half_field, 64, 1)

    def level_input(level):
        source = jnp.where(level < LEVELS // 2, half_field, swapped)
        return jnp.where(lane // NV == level % (LEVELS // 2), source, fixed).astype(BF16)

    def dot(a, b):
        return jnp.dot(a, b, preferred_element_type=F32)

    def cols(q, j):
        return slice(q * HID + j * unit, q * HID + (j + 1) * unit)

    def cell_step(g, j, first=False):
        s = slice(j * unit, (j + 1) * unit)
        c = (0.5 * jnp.tanh(g[0]) + 0.5) * jnp.tanh(g[2] + g[2])
        if not first:
            c = c + (0.5 * jnp.tanh(g[1]) + 0.5) * cell_ref[:, s]
        cell_ref[:, s] = c
        return ((0.25 * jnp.tanh(g[3]) + 0.25) * jnp.tanh(c)).astype(BF16)

    x = level_input(0)
    low_half = cell_step([dot(x, in_w_ref[:, cols(q, 0)]) for q in range(4)], 0, True)
    for q in range(4):
        pend_ref[q] = dot(x, in_w_ref[:, cols(q, 1)])
    cell_ref[:, unit:HID] = jnp.zeros((rows, unit), F32)

    def finish(level, low_half):
        high_half = cell_step([pend_ref[q] for q in range(4)], 1)
        past_ref[level] = jnp.concatenate([low_half, high_half], axis=1)
        return high_half

    def step(level, low_half):
        x = level_input(level)
        for j in range(2):
            for q in range(4):
                feed_ref[j, q] = dot(x, in_w_ref[:, cols(q, j)])
        for j in range(2):
            for q in range(4):
                part_ref[j, q] = feed_ref[j, q] + dot(low_half, hidden_w_ref[0:unit, cols(q, j)])
        high_half = finish(level - 1, low_half)
        g = [
            part_ref[0, q] + dot(high_half, hidden_w_ref[unit:HID, cols(q, 0)]) for q in range(4)
        ]
        new = cell_step(g, 0)
        for q in range(4):
            pend_ref[q] = part_ref[1, q] + dot(high_half, hidden_w_ref[unit:HID, cols(q, 1)])
        return new

    copy.wait()
    out_w = out_w_ref[...].astype(F32)
    out_w = jnp.concatenate([out_w + out_w, jnp.zeros((4, HID), F32)], axis=0).astype(BF16)

    def gains(first, count):
        p = lax.dot_general(
            out_w,
            past_ref[first : first + count].reshape(count * rows, HID),
            (((1,), (1,)), ((), ())),
            preferred_element_type=F32,
        )
        return [p[0:NV, i * rows : (i + 1) * rows] for i in range(count)]

    gain = []
    for level in range(1, LEVELS):
        low_half = step(level, low_half)
        if level % GROUP == 1 and level > GROUP:
            gain += gains(level - 1 - GROUP, GROUP)
    finish(LEVELS - 1, low_half)
    gain += gains(LEVELS - GROUP, GROUP)
    gain = jnp.concatenate(gain, axis=0).T
    out_ref[...] = field + gain.astype(BF16).astype(F32)


def call(kernel, out_shape, *args, kept=(), scratch=(), cost=None):
    placed = len(args)
    args = (*args, *[pltpu.with_memory_space_constraint(a, pltpu.HBM) for a in kept])
    return pl.pallas_call(
        kernel,
        out_shape=out_shape,
        in_specs=[
            pl.BlockSpec(memory_space=pltpu.VMEM if i < placed else pltpu.HBM)
            for i in range(len(args))
        ],
        out_specs=jax.tree.map(lambda _: pl.BlockSpec(memory_space=pltpu.VMEM), out_shape),
        scratch_shapes=list(scratch),
        compiler_params=pltpu.CompilerParams(vmem_limit_bytes=VMEM_LIMIT),
        cost_estimate=cost,
    )(*args)


def like(*shape, dtype=F32):
    return jax.ShapeDtypeStruct(shape, dtype)


ALL = ("z", "y", "c", "x")
ELEM = ("z", "y", "c")


def exchange(to_lower, to_upper, axes):
    size = math.prod(lax.axis_size(a) for a in axes)
    up = [(i, (i + 1) % size) for i in range(size)]
    down = [(j, i) for i, j in up]
    return lax.ppermute(to_upper, axes, up), lax.ppermute(to_lower, axes, down)


def shards(state, assignment, surface, w_state, w_surf, w_hidden, bias, w_out):
    node_rows, node_cols, channels = state.shape
    columns_here = node_rows * node_cols
    slot_count, features = surface.shape
    peers = lax.axis_size("z") * lax.axis_size("y") * lax.axis_size("x")
    block = like(node_rows, node_cols, channels)
    edge = like(2, node_cols, channels)
    moved, to_core, to_chip, spread = call(
        first_kernel,
        (block, edge, edge, like(peers, features, slot_count, dtype=BF16)),
        kept=(state, surface.T),
        scratch=(
            pltpu.VMEM(state.shape, F32),
            pltpu.VMEM((features, slot_count), BF16),
            pltpu.SemaphoreType.DMA((2,)),
        ),
    )
    core = lax.ppermute(to_core, "c", [(0, 1), (1, 0)])
    count = math.prod(lax.axis_size(a) for a in ELEM)
    pairs = [(i, (i + 1) % count) for i in range(1, count, 2)]
    chip = lax.ppermute(to_chip, ELEM, pairs + [(j, i) for i, j in pairs])
    near = lax.all_to_all(spread, ("z", "y", "x"), split_axis=0, concat_axis=0, tiled=True)
    side = like(2 * node_rows + 8, channels)
    g, to_left, to_right = call(
        second_kernel,
        (block, side, side),
        moved,
        core,
        chip,
    )
    left, right = exchange(to_left, to_right, ("x",))
    field = call(third_kernel, block, g, core, chip, left, right)
    near, _ = lax.optimization_barrier((near, field))
    far = lax.ppermute(near, "c", [(0, 1), (1, 0)])
    kept = (assignment.T, w_state, w_surf, w_hidden, bias.reshape(1, 4 * HID))
    prepared = call(
        prepare_kernel,
        (
            like(HID, 4 * HID, dtype=BF16),
            like(LANES, 4 * HID, dtype=BF16),
            like(columns_here, LANES),
            like(columns_here, slot_count, dtype=BF16),
            like(columns_here, LANES, dtype=jnp.int32),
        ),
        near,
        kept=kept,
        scratch=(
            *[pltpu.VMEM(a.shape, a.dtype) for i, a in enumerate(kept) if i != 3],
            pltpu.SemaphoreType.DMA((len(kept),)),
        ),
        cost=pl.CostEstimate(flops=1 << 28, bytes_accessed=4 << 20, transcendentals=0),
    )
    result = call(
        lstm_kernel,
        like(columns_here, channels),
        far,
        field.reshape(columns_here, channels),
        *prepared,
        kept=(w_out.T,),
        scratch=(
            pltpu.VMEM((NV, HID), BF16),
            pltpu.VMEM((columns_here, HID), F32),
            pltpu.VMEM((2, 4, columns_here, HID // 2), F32),
            pltpu.VMEM((4, columns_here, HID // 2), F32),
            pltpu.VMEM((LEVELS, columns_here, HID), BF16),
            pltpu.VMEM((2, 4, columns_here, HID // 2), F32),
            pltpu.SemaphoreType.DMA(()),
        ),
    )
    return result.reshape(node_rows, node_cols, channels)


def solution(mesh):
    devices = mesh.devices
    mesh = jax.sharding.Mesh(devices.reshape(4, 4, 2, 4), ALL)
    placed = (
        P(ELEM, "x", None),
        P(ELEM, "x"),
        P(ALL, None),
        P(),
        P(),
        P(),
        P(),
        P(),
    )
    return jax.shard_map(
        shards, mesh=mesh, in_specs=placed, out_specs=P(ELEM, "x", None), check_vma=False
    )
```

```python
import math

import jax
import jax.numpy as jnp
import numpy as np
from jax import lax
from jax.experimental import pallas as pl
from jax.experimental.pallas import tpu as pltpu
from jax.sharding import PartitionSpec as P

NP = 4
NV = 4
HID = 512
LEVELS = 32
LANES = 128
COURANT = 0.05
F32 = jnp.float32
BF16 = jnp.bfloat16
GROUP = 8
VMEM_LIMIT = 16 << 20


def gll_table():
    nodes = np.array([-1.0, -1.0 / math.sqrt(5.0), 1.0 / math.sqrt(5.0), 1.0])
    width = nodes.shape[0]
    table = np.zeros((width, width))
    for row in range(width):
        for column in range(width):
            if row != column:
                upper = np.prod(
                    [nodes[row] - nodes[other] for other in range(width) if other != row]
                )
                lower = np.prod(
                    [nodes[column] - nodes[other] for other in range(width) if other != column]
                )
                table[row, column] = upper / (lower * (nodes[row] - nodes[column]))
            else:
                table[row, row] = sum(
                    (1.0 / (nodes[row] - nodes[other]) for other in range(width) if other != row)
                )
    return table


D = [[float(v) for v in row] for row in gll_table()]


def winds(f):
    flat = f.reshape(-1, LANES)
    v = lax.broadcasted_iota(jnp.int32, flat.shape, 1) % NV
    one = pltpu.roll(flat, 1, 1)
    two = pltpu.roll(flat, 2, 1)
    three = pltpu.roll(flat, 3, 1)
    back = pltpu.roll(flat, LANES - 1, 1)
    first = jnp.where(v == 0, flat, jnp.where(v == 1, one, jnp.where(v == 2, two, three)))
    second = jnp.where(v == 0, back, jnp.where(v == 1, flat, jnp.where(v == 2, one, two)))
    return first.reshape(f.shape), second.reshape(f.shape)


def along_x(f):
    rows = f.reshape(f.shape[0] // NP, NP, f.shape[1], LANES)
    pieces = []
    for i in range(NP):
        total = D[i][0] * rows[:, 0]
        for k in range(1, NP):
            total = total + D[i][k] * rows[:, k]
        pieces.append(total)
    return jnp.stack(pieces, axis=1).reshape(f.shape)


def along_y(f):
    size = f.shape[1]
    y = lax.broadcasted_iota(jnp.int32, (1, size, LANES), 1) % NP
    total = None
    for shift in range(-(NP - 1), NP):
        factor = jnp.zeros((1, size, LANES), F32)
        for i in range(NP):
            if 0 <= i + shift < NP:
                factor = jnp.where(y == i, D[i][i + shift], factor)
        moved = f if shift == 0 else pltpu.roll(f, (-shift) % size, 1)
        term = factor * moved
        total = term if total is None else total + term
    return total


def average_y(f, left, right):
    size = f.shape[1]
    y = lax.broadcasted_iota(jnp.int32, (1, size, LANES), 1)
    ahead = pltpu.roll(f, size - 1, 1)
    behind = pltpu.roll(f, 1, 1)
    other = jnp.where(y % NP == NP - 1, ahead, jnp.where(y % NP == 0, behind, f))
    other = jnp.where(y == size - 1, right, jnp.where(y == 0, left, other))
    return (f + other) * 0.5


def average_x(f, before, after):
    rows = f.shape[0]
    pieces = []
    for r in range(rows):
        if r % NP == 0:
            other = before if r == 0 else f[r - 1]
            pieces.append((f[r] + other) * 0.5)
        elif r % NP == NP - 1:
            other = after if r == rows - 1 else f[r + 1]
            pieces.append((f[r] + other) * 0.5)
        else:
            pieces.append(f[r])
    return jnp.stack(pieces, axis=0)


def first_kernel(
    state_hbm, surface_hbm, moved_ref, to_core_ref, to_chip_ref, spread_ref, state_ref, surface_ref, arrived
):
    copies = (
        pltpu.make_async_copy(surface_hbm, surface_ref, arrived.at[0]),
        pltpu.make_async_copy(state_hbm, state_ref, arrived.at[1]),
    )
    for copy in copies:
        copy.start()
    copies[0].wait()
    spread_ref[...] = jnp.broadcast_to(surface_ref[...][None], spread_ref.shape)
    copies[1].wait()
    f = state_ref[...]
    wind_x, wind_y = winds(f)
    a = f - COURANT * (wind_x * along_x(f) + wind_y * along_y(f))
    moved_ref[...] = a
    n = a.shape[0]
    first = D[0][1] * a[1] + D[0][2] * a[2] + D[0][3] * ((a[3] + a[4]) * 0.5)
    last = D[3][0] * ((a[n - 4] + a[n - 5]) * 0.5) + D[3][1] * a[n - 3] + D[3][2] * a[n - 2]
    even = lax.axis_index("c") == 0
    to_core_ref[0] = jnp.where(even, a[n - 1], a[0])
    to_core_ref[1] = jnp.where(even, last, first)
    to_chip_ref[0] = jnp.where(even, a[0], a[n - 1])
    to_chip_ref[1] = jnp.where(even, first, last)


def sort_edges(core_ref, chip_ref):
    even = lax.axis_index("c") == 0
    core, chip = core_ref[...], chip_ref[...]
    return jnp.where(even, chip, core), jnp.where(even, core, chip)


def second_kernel(moved_ref, core_ref, chip_ref, g_ref, to_left_ref, to_right_ref):
    before, after = sort_edges(core_ref, chip_ref)
    g = average_x(moved_ref[...], before[0], after[0])
    g_ref[...] = g
    rows, size, _ = g.shape
    middle = (g[:, 3] + g[:, 4]) * 0.5
    to_left_ref[0:rows] = g[:, 0]
    to_left_ref[rows : 2 * rows] = D[0][1] * g[:, 1] + D[0][2] * g[:, 2] + D[0][3] * middle
    to_right_ref[0:rows] = g[:, size - 1]
    to_right_ref[rows : 2 * rows] = (
        D[3][0] * middle + D[3][1] * g[:, size - 3] + D[3][2] * g[:, size - 2]
    )
    up, down = before[1], after[1]
    y = lax.broadcasted_iota(jnp.int32, (size, LANES), 0)
    to_left_ref[2 * rows : 2 * rows + 8] = jnp.where(
        y == 0, up, jnp.where(y == 1, pltpu.roll(down, 1, 0), 0.0)
    )
    to_right_ref[2 * rows : 2 * rows + 8] = jnp.where(
        y == 0, pltpu.roll(up, 1, 0), jnp.where(y == 1, pltpu.roll(down, 2, 0), 0.0)
    )


def third_kernel(g_ref, core_ref, chip_ref, left_ref, right_ref, field_ref):
    before, after = sort_edges(core_ref, chip_ref)
    g = g_ref[...]
    rows, size, _ = g.shape
    left_g = left_ref[0:rows].reshape(rows, 1, LANES)
    right_g = right_ref[0:rows].reshape(rows, 1, LANES)
    f = average_y(g, left_g, right_g)
    tail_l = left_ref[2 * rows : 2 * rows + 8]
    tail_r = right_ref[2 * rows : 2 * rows + 8]
    up = average_y(before[1:2], tail_l[0:1].reshape(1, 1, LANES), tail_r[0:1].reshape(1, 1, LANES))[0]
    down = average_y(after[1:2], tail_l[1:2].reshape(1, 1, LANES), tail_r[1:2].reshape(1, 1, LANES))[0]
    slope_x = average_x(
        along_x(f), D[3][3] * f[0] + up, D[0][0] * f[rows - 1] + down
    )
    other_l = left_ref[rows : 2 * rows].reshape(rows, 1, LANES)
    other_r = right_ref[rows : 2 * rows].reshape(rows, 1, LANES)
    slope_y = average_y(along_y(f), D[3][3] * f + other_l, D[0][0] * f + other_r)
    wind_x, wind_y = winds(f)
    field_ref[...] = f - COURANT * (wind_x * slope_x + wind_y * slope_y)


def pick_owner(table_ref, pick, wanted, surf):
    peers, features, slot_count = table_ref.shape
    lane = lax.broadcasted_iota(jnp.int32, surf.shape, 1)
    for k in range(0, peers, 16):
        found = lax.dot_general(
            pick,
            table_ref[k : k + 16].reshape(16 * features, slot_count),
            (((1,), (1,)), ((), ())),
            preferred_element_type=F32,
        )
        for half in range(2):
            own = wanted == lane // features + (k + 8 * half)
            surf = jnp.where(own, found[:, half * LANES : (half + 1) * LANES], surf)
    return surf


def prepare_kernel(
    near_ref, slots_hbm, state_w_hbm, surf_w_hbm, hidden_w_hbm, bias_hbm,
    hidden_w_ref, in_w_ref, surf_ref, pick_ref, wanted_ref,
    slots_ref, state_w_ref, surf_w_ref, bias_ref, arrived,
):
    pairs = (
        (slots_hbm, slots_ref),
        (state_w_hbm, state_w_ref),
        (surf_w_hbm, surf_w_ref),
        (bias_hbm, bias_ref),
        (hidden_w_hbm, hidden_w_ref),
    )
    copies = [pltpu.make_async_copy(a, b, arrived.at[i]) for i, (a, b) in enumerate(pairs)]
    for copy in copies:
        copy.start()
    rows = surf_ref.shape[0]
    copies[0].wait()
    slots = slots_ref[...]
    slots = jnp.concatenate(
        [jnp.broadcast_to(slots[:, x : x + 1], (8, 2 * LANES)) for x in range(rows // 8)], axis=0
    )
    place = jnp.bitwise_and(slots, 255)
    owner = lax.shift_right_logical(slots[:, :LANES], 8)
    index = jnp.bitwise_or(
        lax.shift_left(lax.shift_right_logical(owner, 3), 2), jnp.bitwise_and(owner, 3)
    )
    here = jnp.bitwise_and(lax.shift_right_logical(owner, 2), 1) == lax.axis_index("c")
    pick = (lax.broadcasted_iota(jnp.int32, place.shape, 1) == place).astype(BF16)
    pick_ref[...] = pick
    wanted_ref[...] = jnp.where(here, -1, index)
    surf_ref[...] = pick_owner(
        near_ref, pick, jnp.where(here, index, -1), jnp.zeros((rows, LANES), F32)
    )
    for copy in copies[1:4]:
        copy.wait()
    row = lax.broadcasted_iota(jnp.int32, (64, NV), 0)
    col = lax.broadcasted_iota(jnp.int32, (64, NV), 1)
    spread = (row % NV == col).astype(BF16)
    in_w_ref[0:64] = jnp.dot(spread, state_w_ref[...], preferred_element_type=F32).astype(BF16)
    bias = bias_ref[...]
    high = bias.astype(BF16).astype(F32)
    rest = bias - high
    mid = rest.astype(BF16).astype(F32)
    low = rest - mid
    r = lax.broadcasted_iota(jnp.int32, (16, 1), 0)
    parts = jnp.where(r == 0, high, jnp.where(r == 1, mid, jnp.where(r == 2, low, 0.0)))
    in_w_ref[64:80] = parts.astype(BF16)
    in_w_ref[80:96] = surf_w_ref[...]
    in_w_ref[96:128] = jnp.zeros((32, 4 * HID), BF16)
    copies[4].wait()


def lstm_kernel(
    far_ref, field_ref, hidden_w_ref, in_w_ref, surf_ref, pick_ref, wanted_ref, out_w_hbm,
    out_ref, out_w_ref, cell_ref, part_ref, pend_ref, past_ref, feed_ref, arrived,
):
    copy = pltpu.make_async_copy(out_w_hbm, out_w_ref, arrived)
    copy.start()
    rows = field_ref.shape[0]
    features = far_ref.shape[1]
    unit = HID // 2
    surf = pick_owner(far_ref, pick_ref[...], wanted_ref[...], surf_ref[...])
    row = lax.broadcasted_iota(jnp.int32, (LANES, LANES), 0)
    col = lax.broadcasted_iota(jnp.int32, (LANES, LANES), 1)
    fold = (col - 80 == row % features).astype(BF16)
    surf = jnp.dot(surf.astype(BF16), fold, preferred_element_type=F32)
    lane = lax.broadcasted_iota(jnp.int32, (rows, LANES), 1)
    fixed = jnp.where((lane >= 64) & (lane < 67), 0.5, 0.5 * surf)
    field = field_ref[...]
    half_field = 0.5 * field.astype(BF16).astype(F32)
    swapped = pltpu.roll(half_field, 64, 1)

    def level_input(level):
        source = jnp.where(level < LEVELS // 2, half_field, swapped)
        return jnp.where(lane // NV == level % (LEVELS // 2), source, fixed).astype(BF16)

    def dot(a, b):
        return jnp.dot(a, b, preferred_element_type=F32)

    def cols(q, j):
        return slice(q * HID + j * unit, q * HID + (j + 1) * unit)

    def cell_step(g, j, first=False):
        s = slice(j * unit, (j + 1) * unit)
        c = (0.5 * jnp.tanh(g[0]) + 0.5) * jnp.tanh(g[2] + g[2])
        if not first:
            c = c + (0.5 * jnp.tanh(g[1]) + 0.5) * cell_ref[:, s]
        cell_ref[:, s] = c
        return ((0.25 * jnp.tanh(g[3]) + 0.25) * jnp.tanh(c)).astype(BF16)

    x = level_input(0)
    low_half = cell_step([dot(x, in_w_ref[:, cols(q, 0)]) for q in range(4)], 0, True)
    for q in range(4):
        pend_ref[q] = dot(x, in_w_ref[:, cols(q, 1)])
    cell_ref[:, unit:HID] = jnp.zeros((rows, unit), F32)

    def finish(level, low_half):
        high_half = cell_step([pend_ref[q] for q in range(4)], 1)
        past_ref[level] = jnp.concatenate([low_half, high_half], axis=1)
        return high_half

    def step(level, low_half):
        x = level_input(level)
        for j in range(2):
            for q in range(4):
                feed_ref[j, q] = dot(x, in_w_ref[:, cols(q, j)])
        for j in range(2):
            for q in range(4):
                part_ref[j, q] = feed_ref[j, q] + dot(low_half, hidden_w_ref[0:unit, cols(q, j)])
        high_half = finish(level - 1, low_half)
        g = [
            part_ref[0, q] + dot(high_half, hidden_w_ref[unit:HID, cols(q, 0)]) for q in range(4)
        ]
        new = cell_step(g, 0)
        for q in range(4):
            pend_ref[q] = part_ref[1, q] + dot(high_half, hidden_w_ref[unit:HID, cols(q, 1)])
        return new

    copy.wait()
    out_w = out_w_ref[...].astype(F32)
    out_w = jnp.concatenate([out_w + out_w, jnp.zeros((4, HID), F32)], axis=0).astype(BF16)

    def gains(first, count):
        p = lax.dot_general(
            out_w,
            past_ref[first : first + count].reshape(count * rows, HID),
            (((1,), (1,)), ((), ())),
            preferred_element_type=F32,
        )
        return [p[0:NV, i * rows : (i + 1) * rows] for i in range(count)]

    gain = []
    for level in range(1, LEVELS):
        low_half = step(level, low_half)
        if level % GROUP == 1 and level > GROUP:
            gain += gains(level - 1 - GROUP, GROUP)
    finish(LEVELS - 1, low_half)
    gain += gains(LEVELS - GROUP, GROUP)
    gain = jnp.concatenate(gain, axis=0).T
    out_ref[...] = field + gain.astype(BF16).astype(F32)


def call(kernel, out_shape, *args, kept=(), scratch=(), cost=None):
    placed = len(args)
    args = (*args, *[pltpu.with_memory_space_constraint(a, pltpu.HBM) for a in kept])
    return pl.pallas_call(
        kernel,
        out_shape=out_shape,
        in_specs=[
            pl.BlockSpec(memory_space=pltpu.VMEM if i < placed else pltpu.HBM)
            for i in range(len(args))
        ],
        out_specs=jax.tree.map(lambda _: pl.BlockSpec(memory_space=pltpu.VMEM), out_shape),
        scratch_shapes=list(scratch),
        compiler_params=pltpu.CompilerParams(vmem_limit_bytes=VMEM_LIMIT),
        cost_estimate=cost,
    )(*args)


def like(*shape, dtype=F32):
    return jax.ShapeDtypeStruct(shape, dtype)


ALL = ("z", "y", "c", "x")
ELEM = ("z", "y", "c")


def exchange(to_lower, to_upper, axes):
    size = math.prod(lax.axis_size(a) for a in axes)
    up = [(i, (i + 1) % size) for i in range(size)]
    down = [(j, i) for i, j in up]
    return lax.ppermute(to_upper, axes, up), lax.ppermute(to_lower, axes, down)


def shards(state, assignment, surface, w_state, w_surf, w_hidden, bias, w_out):
    node_rows, node_cols, channels = state.shape
    columns_here = node_rows * node_cols
    slot_count, features = surface.shape
    peers = lax.axis_size("z") * lax.axis_size("y") * lax.axis_size("x")
    block = like(node_rows, node_cols, channels)
    edge = like(2, node_cols, channels)
    moved, to_core, to_chip, spread = call(
        first_kernel,
        (block, edge, edge, like(peers, features, slot_count, dtype=BF16)),
        kept=(state, surface.T),
        scratch=(
            pltpu.VMEM(state.shape, F32),
            pltpu.VMEM((features, slot_count), BF16),
            pltpu.SemaphoreType.DMA((2,)),
        ),
    )
    core = lax.ppermute(to_core, "c", [(0, 1), (1, 0)])
    count = math.prod(lax.axis_size(a) for a in ELEM)
    pairs = [(i, (i + 1) % count) for i in range(1, count, 2)]
    chip = lax.ppermute(to_chip, ELEM, pairs + [(j, i) for i, j in pairs])
    near = lax.all_to_all(spread, ("z", "y", "x"), split_axis=0, concat_axis=0, tiled=True)
    side = like(2 * node_rows + 8, channels)
    g, to_left, to_right = call(
        second_kernel,
        (block, side, side),
        moved,
        core,
        chip,
    )
    left, right = exchange(to_left, to_right, ("x",))
    field = call(third_kernel, block, g, core, chip, left, right)
    near, _ = lax.optimization_barrier((near, left))
    far = lax.ppermute(near, "c", [(0, 1), (1, 0)])
    kept = (assignment.T, w_state, w_surf, w_hidden, bias.reshape(1, 4 * HID))
    prepared = call(
        prepare_kernel,
        (
            like(HID, 4 * HID, dtype=BF16),
            like(LANES, 4 * HID, dtype=BF16),
            like(columns_here, LANES),
            like(columns_here, slot_count, dtype=BF16),
            like(columns_here, LANES, dtype=jnp.int32),
        ),
        near,
        kept=kept,
        scratch=(
            *[pltpu.VMEM(a.shape, a.dtype) for i, a in enumerate(kept) if i != 3],
            pltpu.SemaphoreType.DMA((len(kept),)),
        ),
        cost=pl.CostEstimate(flops=1 << 28, bytes_accessed=4 << 20, transcendentals=0),
    )
    result = call(
        lstm_kernel,
        like(columns_here, channels),
        far,
        field.reshape(columns_here, channels),
        *prepared,
        kept=(w_out.T,),
        scratch=(
            pltpu.VMEM((NV, HID), BF16),
            pltpu.VMEM((columns_here, HID), F32),
            pltpu.VMEM((2, 4, columns_here, HID // 2), F32),
            pltpu.VMEM((4, columns_here, HID // 2), F32),
            pltpu.VMEM((LEVELS, columns_here, HID), BF16),
            pltpu.VMEM((2, 4, columns_here, HID // 2), F32),
            pltpu.SemaphoreType.DMA(()),
        ),
    )
    return result.reshape(node_rows, node_cols, channels)


def solution(mesh):
    devices = mesh.devices
    mesh = jax.sharding.Mesh(devices.reshape(4, 4, 2, 4), ALL)
    placed = (
        P(ELEM, "x", None),
        P(ELEM, "x"),
        P(ALL, None),
        P(),
        P(),
        P(),
        P(),
        P(),
    )
    return jax.shard_map(
        shards, mesh=mesh, in_specs=placed, out_specs=P(ELEM, "x", None), check_vma=False
    )
```
